256 devices in a mesh: row: 16 (over y, z_lo, core), col: 16 (over x, z_hi).
Axes of the slice: x: 4, y: 4, z: 8 (z_hi: 4, z_lo: 2; z = z_hi * 2 + z_lo), core: 2. Of those that a mesh axis runs over, the one named last changes fastest.
Arguments:
- node_features: bfloat16 [65536, 512], P('col', 'row'), may hold values from -6 to 6
- layer_weight: bfloat16 [512, 512], replicated, may hold values from -0.25 to 0.25
- tile_values: bfloat16 [16, 16, 96, 128, 128], P('row', 'col')
- tile_coords: int32 [16, 16, 96, 2], P('row', 'col'), may hold values from 0 to 31, as said below
- tile_count: int32 [16, 16], P('row', 'col'), may hold values from 32 to 96, as said below
- cotangent: bfloat16 [65536, 512], P(('row', 'col')), may hold values from -6 to 6
Outputs:
- hidden: bfloat16 [65536, 512], P(('row', 'col'))
- grad_weight: float32 [512, 512], replicated
- grad_features: bfloat16 [65536, 512], P('col', 'row')
The draws below stay inside these ranges and needn't reach their ends.
Inputs may be any that keep to these rules, and one draw needn't show every extreme that they name: `tile_coords`: entry 0 of a slot is its destination tile within the destination block, below 32; entry 1 its source tile within the source block, below 32; the slots of one block pair name distinct positions. `tile_count`: slots at or beyond the count hold arbitrary tiles that are not part of the adjacency.
All inputs are finite; a program needn't handle non-finite values.
Results may differ from the reference program's by a relative error of at most 0.0054.
Values may be sent and summed in bfloat16 or wider, within the bound.
A program may use at most 128 MiB of HBM per device.

```python
import math
import jax
import jax.numpy as jnp
from jax import lax

F = 512
TILE = 128
NODE_DEV = 256
TILES_DEV = 96
NODES = 65536
BLOCK_R = 4096
BLOCK_C = 4096
N_ROW = 16
N_COL = 16


def draw_tile_values(key, part):
    key = jax.random.fold_in(key, 11)
    key_live, key_size = jax.random.split(key, 2)
    shape = (N_ROW, N_COL, TILES_DEV, TILE, TILE)
    live = (jax.random.uniform(key_live, shape, jnp.float32) < 0.35).astype(jnp.float32)
    magnitude = jnp.exp(jax.random.uniform(key_size, shape, jnp.float32, math.log(0.5), math.log(2.0)))
    second = 1.2
    scale = (0.35 * second * TILES_DEV * TILE * TILE / NODE_DEV) ** (-0.5)
    return (live * magnitude * scale).astype(jnp.bfloat16)


def draw_tile_coords(key, part):
    key = jax.random.fold_in(key, 12)
    dest_tiles = NODE_DEV * N_COL // TILE
    source_tiles = NODE_DEV * N_ROW // TILE
    positions = dest_tiles * source_tiles
    keys = jax.random.split(key, N_ROW * N_COL)
    chosen = jax.vmap(lambda one_key: jax.random.permutation(one_key, positions)[:TILES_DEV])(keys)
    chosen = chosen.astype(jnp.int32)
    coords = jnp.stack([chosen // source_tiles, chosen % source_tiles], axis=-1)
    return coords.reshape(N_ROW, N_COL, TILES_DEV, 2).astype(jnp.int32)


def draw_tile_count(key, part):
    key = jax.random.fold_in(key, 13)
    counts = jax.random.randint(key, (N_ROW, N_COL), TILES_DEV // 3, TILES_DEV + 1, jnp.int32)
    counts = counts.at[0, 0].set(TILES_DEV)
    counts = counts.at[0, 1].set(TILES_DEV // 3)
    return counts


def level_of(key, shape, shards, least, top_value):
    loudness = 1.0
    for position, blocks in shards:
        draws = jax.random.uniform(jax.random.fold_in(jax.random.fold_in(key, 6), position), (blocks,), jnp.float32, least / len(shards), top_value / len(shards))
        loudness = loudness * jnp.repeat(jnp.exp(draws), shape[position] // blocks).reshape((-1,) + (1,) * (len(shape) - 1 - position))
    return loudness


def bell_draw(stream_key, dims, deviation, bound, cuts=(), kind=jnp.bfloat16):
    drawn = jax.random.normal(stream_key, dims, jnp.float32) * deviation
    if len(cuts) > 0:
        drawn = level_of(stream_key, dims, cuts, -0.22, 0.18) * drawn
    return jnp.clip(drawn, min=-bound, max=bound).astype(kind)


def setup_inputs(seed: int = 0) -> dict:
    splits = jax.random.split(jax.random.key(seed), 7)
    node_features = bell_draw(splits[0], (NODES, F), 1.0, 6.0, ((0, 16), (1, 16)))
    layer_weight = bell_draw(splits[1], (F, F), F ** -0.5, 0.25)
    tile_values = draw_tile_values(jax.random.fold_in(splits[6], 71), 0)
    tile_coords = draw_tile_coords(jax.random.fold_in(splits[6], 71), 0)
    tile_count = draw_tile_count(jax.random.fold_in(splits[6], 71), 0)
    cotangent = bell_draw(splits[5], (NODES, F), 1.0, 6.0, ((0, 256),))
    return dict(node_features=node_features, layer_weight=layer_weight, tile_values=tile_values, tile_coords=tile_coords, tile_count=tile_count, cotangent=cotangent)


def forward_block(tiles, coords, live_count, source_rows):
    slots = tiles.shape[0]
    gathered_rows = source_rows.reshape(BLOCK_C // TILE, TILE, F)[coords[:, 1]]
    product = jnp.einsum('tab,tbk->tak', tiles.astype(jnp.float32), gathered_rows.astype(jnp.float32))
    is_live = jnp.arange(slots) < live_count
    product = jnp.where(is_live[:, None, None], product, jnp.float32(0.0))
    summed = jax.ops.segment_sum(product, coords[:, 0], num_segments=BLOCK_R // TILE)
    return summed.reshape(BLOCK_R, F)


def backward_block(tiles, coords, live_count, dest_rows):
    slots = tiles.shape[0]
    gathered_rows = dest_rows.reshape(BLOCK_R // TILE, TILE, F)[coords[:, 0]]
    product = jnp.einsum('tab,tak->tbk', tiles.astype(jnp.float32), gathered_rows.astype(jnp.float32))
    is_live = jnp.arange(slots) < live_count
    product = jnp.where(is_live[:, None, None], product, jnp.float32(0.0))
    summed = jax.ops.segment_sum(product, coords[:, 1], num_segments=BLOCK_C // TILE)
    return summed.reshape(BLOCK_C, F)


def reference(node_features, layer_weight, tile_values, tile_coords, tile_count, cotangent):
    pairs = N_ROW * N_COL

    def forward_pair(index, totals):
        dest = (index // N_COL).astype(jnp.int32)
        source = (index % N_COL).astype(jnp.int32)
        source_rows = lax.dynamic_slice_in_dim(node_features, (source * BLOCK_C).astype(jnp.int32), BLOCK_C, 0)
        term = forward_block(tile_values[dest, source], tile_coords[dest, source], tile_count[dest, source], source_rows)
        current = lax.dynamic_slice_in_dim(totals, (dest * BLOCK_R).astype(jnp.int32), BLOCK_R, 0)
        return lax.dynamic_update_slice_in_dim(totals, current + term, (dest * BLOCK_R).astype(jnp.int32), 0)

    summed = lax.fori_loop(0, pairs, forward_pair, jnp.zeros((NODES, F), jnp.float32))
    aggregated = summed.astype(jnp.bfloat16)
    pre_act = jnp.dot(aggregated, layer_weight, preferred_element_type=jnp.float32)
    hidden = jax.nn.elu(pre_act).astype(jnp.bfloat16)
    slope = jnp.where(pre_act > 0, jnp.float32(1.0), jnp.exp(jnp.minimum(pre_act, 0.0)))
    grad_pre = (cotangent.astype(jnp.float32) * slope).astype(jnp.bfloat16)
    grad_weight = jnp.dot(aggregated.T, grad_pre, preferred_element_type=jnp.float32)
    grad_agg = jnp.dot(grad_pre, layer_weight.T, preferred_element_type=jnp.float32).astype(jnp.bfloat16)

    def backward_pair(index, totals):
        dest = (index // N_COL).astype(jnp.int32)
        source = (index % N_COL).astype(jnp.int32)
        dest_rows = lax.dynamic_slice_in_dim(grad_agg, (dest * BLOCK_R).astype(jnp.int32), BLOCK_R, 0)
        term = backward_block(tile_values[dest, source], tile_coords[dest, source], tile_count[dest, source], dest_rows)
        current = lax.dynamic_slice_in_dim(totals, (source * BLOCK_C).astype(jnp.int32), BLOCK_C, 0)
        return lax.dynamic_update_slice_in_dim(totals, current + term, (source * BLOCK_C).astype(jnp.int32), 0)

    back = lax.fori_loop(0, pairs, backward_pair, jnp.zeros((NODES, F), jnp.float32))
    return hidden, grad_weight, back.astype(jnp.bfloat16)
```

```python
import jax
import jax.numpy as jnp
from jax import lax
from jax.experimental import pallas as pl
from jax.experimental.pallas import tpu as pltpu
from jax.sharding import PartitionSpec as P

MESH = pl.DeviceIdType.MESH
BF16 = jnp.bfloat16
F32 = jnp.float32

SLOTS = 96
TILES = 32
TILE = 128
WIDTH = 512
CHUNK = 256
UNROLL = 4
WIRES = 144

NT = (((1,), (1,)), ((), ()))
NN = (((1,), (0,)), ((), ()))
TN = (((0,), (0,)), ((), ()))


def dot(a, b, dims):
    return lax.dot_general(a, b, dims, preferred_element_type=F32)


def order_table(main, other, live):
    index = jnp.arange(SLOTS, dtype=jnp.int32)
    key = jnp.where(live, main * 64 + other, 4096 + index)
    before = key[None, :] < key[:, None]
    rank = jnp.sum(before, axis=1, dtype=jnp.int32)
    same = before & live[None, :] & (main[None, :] == main[:, None])
    first = jnp.logical_not(jnp.any(same, axis=1)).astype(jnp.int32)
    places = rank[None, :] == index[:, None]
    facts = jnp.stack([index, jnp.where(live, other, 0), first])
    ordered = jnp.sum(jnp.where(places[None], facts[:, None, :], 0), axis=2, dtype=jnp.int32)
    upto = jnp.sum(live[None, :] & (main[None, :] <= index[:, None]), axis=1, dtype=jnp.int32)
    count = jnp.sum(live[None, :] & (main[None, :] == index[:, None]), axis=1, dtype=jnp.int32)
    last = jnp.maximum(upto - 1, 0)
    return jnp.concatenate([ordered, last[None], count[None]])


def kernel(
    table, xt, tiles, weight, cot, hid, gw, gft,
    xg0, xg1, run, ys, yown, xrl, xrr, xinl, xinr, zs, zrl, zrr, zinl, zinr,
    aggt, gpre, gg0, gg1, bown, bsend, cin, yb, yrl, yrr, yinl, yinr, zout, zpin,
    gsum, gout, rin_c, rin_z, rin_y, rin_x, rin_h, send_sem, recv_sem,
):
    xg, gg = (xg0, xg1), (gg0, gg1)
    r = lax.axis_index("row")
    c = lax.axis_index("col")
    y, zl, core = r // 4, (r // 2) % 2, r % 2
    x, zh = c // 4, c % 4

    def turn(v, by):
        return (v + by) % 4

    def at_y(by):
        return (turn(y, by) * 4 + r % 4, c)

    def at_x(by):
        return (r, turn(x, by) * 4 + zh)

    def at_h(by):
        return (r, x * 4 + turn(zh, by))

    at_z = (r + 2 - 4 * zl, c)
    at_core = (r + 1 - 2 * core, c)

    barrier = pltpu.get_barrier_semaphore()
    peers = [at_z, at_core] + [f(by) for f in (at_y, at_x, at_h) for by in (1, 2, 3)]
    for peer in peers:
        pl.semaphore_signal(barrier, inc=1, device_id=peer, device_id_type=MESH)
    pl.semaphore_wait(barrier, len(peers))

    started = []

    def send(src, dst, peer):
        i = len(started)
        copy = pltpu.make_async_remote_copy(
            src_ref=src, dst_ref=dst, send_sem=send_sem.at[i], recv_sem=recv_sem.at[i],
            device_id=peer, device_id_type=MESH,
        )
        copy.start()
        started.append(copy)
        return copy

    def gather_row(k):
        def whole(owner):
            return xg[k].at[owner]

        def part(owner, h):
            return xg[k].at[owner, pl.ds(16 * h, 16)]

        rz = at_z[0]
        to_z = send(xt.at[k], whole(r), at_z)
        up = send(xt.at[k], whole(r), at_y(1))
        down = send(xt.at[k], whole(r), at_y(3))
        inside = [send(xt.at[k], whole(r), at_core)]
        xg[k][r] = xt[k]
        yield
        to_z.wait_recv()
        up_z = send(whole(rz), whole(rz), at_y(1))
        down_z = send(whole(rz), whole(rz), at_y(3))
        inside.append(send(whole(rz), whole(rz), at_core))
        yield
        relays = []
        for copy, by, base in ((up, 3, r), (down, 1, r), (up_z, 3, rz), (down_z, 1, rz)):
            owner = turn(y, by) * 4 + base % 4
            copy.wait_recv()
            if by == 3:
                relays.append(send(part(owner, 0), part(owner, 0), at_y(1)))
            else:
                relays.append(send(part(owner, 1), part(owner, 1), at_y(3)))
            inside.append(send(whole(owner), whole(owner), at_core))
        yield
        for base, pair in ((r, relays[:2]), (rz, relays[2:])):
            owner = turn(y, 2) * 4 + base % 4
            for copy in pair:
                copy.wait_recv()
            inside.append(send(whole(owner), whole(owner), at_core))
        yield
        for copy in inside:
            copy.wait_recv()
        yield

    def sweep(load, dims, base):
        def step(u, total):
            for v in range(UNROLL):
                t = u * UNROLL + v
                block = tiles[table[base, t]]
                product = dot(load(table[base + 1, t]), block, dims)
                total = jnp.where(table[base + 2, t] > 0, product, total + product)
                run[t] = total
            return total

        lax.fori_loop(0, SLOTS // UNROLL, step, jnp.zeros((CHUNK, TILE), F32))

    def segment(base, d):
        return jnp.where(table[base + 4, d] > 0, run[table[base + 3, d]], 0.0)

    def loop(n, f):
        def step(i, carry):
            f(i)
            return carry

        lax.fori_loop(0, n, step, 0)

    def reduce_col(k):
        sweep(lambda s: xg[k][:, s].reshape(CHUNK, TILE), NT, 0)
        far, nxt, prv, own = (8 * turn(x, by) for by in (2, 1, 3, 0))

        def rounded(base):
            def one(i):
                ys[k, base + i] = segment(0, base + i).astype(BF16)

            loop(8, one)

        rounded(far)
        relay_l = send(ys.at[k, pl.ds(far, 4)], xrl.at[k], at_x(1))
        relay_r = send(ys.at[k, pl.ds(far + 4, 4)], xrr.at[k], at_x(3))
        rounded(nxt)
        plain_l = send(ys.at[k, pl.ds(nxt + 4, 4)], xinl.at[k, pl.ds(4, 4)], at_x(1))
        rounded(prv)
        plain_r = send(ys.at[k, pl.ds(prv, 4)], xinr.at[k, pl.ds(0, 4)], at_x(3))

        def kept(i):
            yown[k, i] = segment(0, own + i)

        loop(8, kept)
        yield

        def passed_l(i):
            ys[k, nxt + i] = (ys[k, nxt + i].astype(F32) + xrl[k, i].astype(F32)).astype(BF16)

        def passed_r(i):
            ys[k, prv + 4 + i] = (ys[k, prv + 4 + i].astype(F32) + xrr[k, i].astype(F32)).astype(BF16)

        relay_l.wait_recv()
        loop(4, passed_l)
        sum_l = send(ys.at[k, pl.ds(nxt, 4)], xinl.at[k, pl.ds(0, 4)], at_x(1))
        relay_r.wait_recv()
        loop(4, passed_r)
        sum_r = send(ys.at[k, pl.ds(prv + 4, 4)], xinr.at[k, pl.ds(4, 4)], at_x(3))
        yield
        for copy in (plain_l, plain_r, sum_l, sum_r):
            copy.wait_recv()

        def summed(i):
            total = yown[k, i] + xinl[k, i].astype(F32) + xinr[k, i].astype(F32)
            yown[k, i] = total
            zs[k, i] = total.astype(BF16)

        loop(8, summed)
        far, nxt, prv, own = (2 * turn(zh, by) for by in (2, 1, 3, 0))
        relay_l = send(zs.at[k, far], zrl.at[k], at_h(1))
        relay_r = send(zs.at[k, far + 1], zrr.at[k], at_h(3))
        plain_l = send(zs.at[k, nxt + 1], zinl.at[k, 1], at_h(1))
        plain_r = send(zs.at[k, prv], zinr.at[k, 0], at_h(3))
        yield
        relay_l.wait_recv()
        zs[k, nxt] = (yown[k, nxt] + zrl[k].astype(F32)).astype(BF16)
        sum_l = send(zs.at[k, nxt], zinl.at[k, 0], at_h(1))
        relay_r.wait_recv()
        zs[k, prv + 1] = (yown[k, prv + 1] + zrr[k].astype(F32)).astype(BF16)
        sum_r = send(zs.at[k, prv + 1], zinr.at[k, 1], at_h(3))
        yield
        for copy in (plain_l, plain_r, sum_l, sum_r):
            copy.wait_recv()
        for i in range(2):
            total = yown[k, own + i] + zinl[k, i].astype(F32) + zinr[k, i].astype(F32)
            aggt[k, :, i * TILE : (i + 1) * TILE] = total.astype(BF16)
        yield

    def gather_col(k):
        def whole(by_x, by_h):
            return gg[k].at[pl.ds(2 * (turn(x, by_x) * 4 + turn(zh, by_h)), 2)]

        def half(by_h, i):
            return gg[k].at[2 * (x * 4 + turn(zh, by_h)) + i]

        right, left = {}, {}

        def along_x(by_h):
            right[by_h] = send(whole(0, by_h), whole(0, by_h), at_x(1))
            left[by_h] = send(whole(0, by_h), whole(0, by_h), at_x(3))

        up = send(whole(0, 0), whole(0, 0), at_h(1))
        down = send(whole(0, 0), whole(0, 0), at_h(3))
        yield
        along_x(0)
        yield
        up.wait_recv()
        relay_up = send(half(3, 0), half(3, 0), at_h(1))
        along_x(3)
        down.wait_recv()
        relay_down = send(half(1, 1), half(1, 1), at_h(3))
        along_x(1)
        yield
        relay_up.wait_recv()
        relay_down.wait_recv()
        along_x(2)
        yield
        relays = []
        for by_h in (0, 3, 1, 2):
            right[by_h].wait_recv()
            if by_h in (0, 1):
                relays.append(send(whole(3, by_h), whole(3, by_h), at_x(1)))
            left[by_h].wait_recv()
            if by_h in (2, 3):
                relays.append(send(whole(1, by_h), whole(1, by_h), at_x(3)))
        yield
        for copy in relays:
            copy.wait_recv()
        yield

    def reduce_row(k):
        sweep(lambda d: gg[k][d], NN, 5)

        def split(s):
            both = segment(5, s).reshape(8, 2, 16, TILE)
            bown[k, :, s] = jnp.where(core == 0, both[:, 0], both[:, 1])
            bsend[k, :, s] = jnp.where(core == 0, both[:, 1], both[:, 0]).astype(BF16)

        loop(TILES, split)
        far, nxt, prv, own = (2 * turn(y, by) for by in (2, 1, 3, 0))
        inside = [send(bsend.at[k, pl.ds(b, 2)], cin.at[k, pl.ds(b, 2)], at_core) for b in (far, nxt, prv, own)]
        yield

        def joined(base):
            for i in range(2):
                def rows(h):
                    cut = pl.ds(h * 8, 8)
                    total = bown[k, base + i, cut] + cin[k, base + i, cut].astype(F32)
                    bown[k, base + i, cut] = total
                    yb[k, base + i, cut] = total.astype(BF16)

                loop(4, rows)

        inside[0].wait_recv()
        joined(far)
        relay_l = send(yb.at[k, far], yrl.at[k], at_y(1))
        relay_r = send(yb.at[k, far + 1], yrr.at[k], at_y(3))
        inside[1].wait_recv()
        joined(nxt)
        plain_l = send(yb.at[k, nxt + 1], yinl.at[k, 1], at_y(1))
        inside[2].wait_recv()
        joined(prv)
        plain_r = send(yb.at[k, prv], yinr.at[k, 0], at_y(3))
        inside[3].wait_recv()
        joined(own)
        yield

        def passed(at, came):
            def rows(h):
                cut = pl.ds(h * 8, 8)
                yb[k, at, cut] = (bown[k, at, cut] + came[k, cut].astype(F32)).astype(BF16)

            loop(4, rows)

        relay_l.wait_recv()
        passed(nxt, yrl)
        sum_l = send(yb.at[k, nxt], yinl.at[k, 0], at_y(1))
        relay_r.wait_recv()
        passed(prv + 1, yrr)
        sum_r = send(yb.at[k, prv + 1], yinr.at[k, 1], at_y(3))
        yield
        for copy in (plain_l, plain_r, sum_l, sum_r):
            copy.wait_recv()

        def total_of(i, cut):
            return bown[k, own + i, cut] + yinl[k, i, cut].astype(F32) + yinr[k, i, cut].astype(F32)

        def leaving(h):
            cut = pl.ds(h * 8, 8)
            zout[k, cut] = total_of(1 - zl, cut).astype(BF16)

        loop(4, leaving)
        to_z = send(zout.at[k], zpin.at[k], at_z)
        yield
        to_z.wait_recv()

        def final(h):
            cut = pl.ds(h * 8, 8)
            gft[k, cut] = (total_of(zl, cut) + zpin[k, cut].astype(F32)).astype(BF16)

        loop(4, final)
        yield

    def reduce_weight():
        rows_z = pl.multiple_of(128 * zl, 128)
        rows_y = pl.multiple_of(rows_z + 32 * y, 32)
        rows_x = pl.multiple_of(rows_y + 8 * x, 8)
        lanes = pl.multiple_of(128 * zh, 128)
        copy = send(gsum.at[1 - core], rin_c, at_core)
        yield
        copy.wait_recv()
        gsum[core] += rin_c[...]
        copy = send(gsum.at[core, pl.ds(pl.multiple_of(128 - rows_z, 128), 128)], rin_z, at_z)
        yield
        copy.wait_recv()
        gsum[core, pl.ds(rows_z, 128)] += rin_z[...]
        copies = [
            send(
                gsum.at[core, pl.ds(pl.multiple_of(rows_z + 32 * turn(y, by), 32), 32)],
                rin_y.at[by - 1], at_y(by),
            )
            for by in (1, 2, 3)
        ]
        yield
        for copy in copies:
            copy.wait_recv()
        gsum[core, pl.ds(rows_y, 32)] += rin_y[0] + rin_y[1] + rin_y[2]
        copies = [
            send(
                gsum.at[core, pl.ds(pl.multiple_of(rows_y + 8 * turn(x, by), 8), 8)],
                rin_x.at[by - 1], at_x(by),
            )
            for by in (1, 2, 3)
        ]
        yield
        for copy in copies:
            copy.wait_recv()
        gsum[core, pl.ds(rows_x, 8)] += rin_x[0] + rin_x[1] + rin_x[2]
        copies = [
            send(
                gsum.at[core, pl.ds(rows_x, 8), pl.ds(pl.multiple_of(128 * turn(zh, by), 128), 128)],
                rin_h.at[by - 1], at_h(by),
            )
            for by in (1, 2, 3)
        ]
        yield
        for copy in copies:
            copy.wait_recv()
        corner = (core, pl.ds(rows_x, 8), pl.ds(lanes, 128))
        gout[corner] = gsum[corner] + rin_h[0] + rin_h[1] + rin_h[2]
        for cut, where in (
            (corner, [at_h(by) for by in (1, 2, 3)]),
            ((core, pl.ds(rows_x, 8)), [at_x(by) for by in (1, 2, 3)]),
            ((core, pl.ds(rows_y, 32)), [at_y(by) for by in (1, 2, 3)]),
            ((core, pl.ds(rows_z, 128)), [at_z]),
            ((core,), [at_core]),
        ):
            copies = [send(gout.at[cut], gout.at[cut], peer) for peer in where]
            yield
            for copy in copies:
                copy.wait_recv()
        for k in range(2):
            gw[:, k] = gout[k].reshape(16, 16, WIDTH)
        yield

    rows = [gather_row(k) for k in range(2)]
    cols = [reduce_col(k) for k in range(2)]
    for _ in range(3):
        next(rows[0])
    next(rows[1])
    next(rows[0])
    next(rows[0])
    next(cols[0])
    for _ in range(2):
        next(rows[1])
    next(cols[0])
    for _ in range(2):
        next(rows[1])
    next(cols[1])
    next(cols[0])
    next(cols[1])
    next(cols[0])
    next(cols[0])
    for _ in range(3):
        next(cols[1])

    for n in range(2):
        cut = slice(n * CHUNK, (n + 1) * CHUNK)
        pre = jnp.zeros((CHUNK, CHUNK), F32)
        for k in range(2):
            pre += dot(aggt[k], weight[:, k, :, cut].reshape(CHUNK, CHUNK), TN)
        low = jnp.exp(jnp.minimum(pre, 0.0))
        hid[:, cut] = jnp.where(pre > 0, pre, low - 1.0).astype(BF16)
        slope = jnp.where(pre > 0, 1.0, low)
        gpre[:, cut] = (cot[:, cut].astype(F32) * slope).astype(BF16)

    def grad_agg(k):
        made = dot(weight[:, k].reshape(CHUNK, WIDTH), gpre[...], NT).astype(BF16)
        for i in range(2):
            gg[k][2 * c + i] = made[:, i * TILE : (i + 1) * TILE]

    cols = [gather_col(k) for k in range(2)]
    rows = [reduce_row(k) for k in range(2)]
    total = reduce_weight()
    grad_agg(0)
    next(cols[0])
    next(cols[0])
    grad_agg(1)
    next(cols[1])
    for k in range(2):
        gsum[k] = dot(aggt[k], gpre[...], NN)
    next(total)
    next(cols[0])
    next(cols[0])
    next(total)
    next(cols[0])
    next(cols[1])
    next(cols[1])
    next(cols[1])
    next(total)
    next(cols[0])
    next(rows[0])
    next(total)
    next(cols[1])
    next(rows[0])
    next(total)
    next(rows[0])
    next(total)
    next(cols[1])
    next(rows[1])
    next(total)
    next(rows[0])
    next(rows[1])
    next(total)
    next(rows[0])
    next(rows[1])
    next(total)
    next(rows[1])
    next(total)
    next(rows[1])
    next(total)
    for copy in started:
        copy.wait_send()


def body(node_features, layer_weight, tile_values, tile_coords, tile_count, cotangent):
    coords = tile_coords[0, 0]
    live = jnp.arange(SLOTS) < tile_count[0, 0]
    table = jnp.concatenate(
        [order_table(coords[:, 0], coords[:, 1], live), order_table(coords[:, 1], coords[:, 0], live)]
    )
    xt = node_features.reshape(TILES, TILE, 2, 16).transpose(2, 0, 3, 1)
    vmem = pl.BlockSpec(memory_space=pltpu.VMEM)
    slab = (CHUNK, TILE)
    bits = (TILES, 16, TILE)
    hid, gw, gft = pl.pallas_call(
        kernel,
        out_shape=[
            jax.ShapeDtypeStruct((CHUNK, WIDTH), BF16),
            jax.ShapeDtypeStruct((16, 2, 16, WIDTH), F32),
            jax.ShapeDtypeStruct((2,) + bits, BF16),
        ],
        in_specs=[pl.BlockSpec(memory_space=pltpu.SMEM)] + [vmem] * 4,
        out_specs=[vmem] * 3,
        scratch_shapes=[
            pltpu.VMEM((16,) + bits, BF16),
            pltpu.VMEM((16,) + bits, BF16),
            pltpu.VMEM((SLOTS,) + slab, F32),
            pltpu.VMEM((2, TILES) + slab, BF16),
            pltpu.VMEM((2, 8) + slab, F32),
            pltpu.VMEM((2, 4) + slab, BF16),
            pltpu.VMEM((2, 4) + slab, BF16),
            pltpu.VMEM((2, 8) + slab, BF16),
            pltpu.VMEM((2, 8) + slab, BF16),
            pltpu.VMEM((2, 8) + slab, BF16),
            pltpu.VMEM((2,) + slab, BF16),
            pltpu.VMEM((2,) + slab, BF16),
            pltpu.VMEM((2, 2) + slab, BF16),
            pltpu.VMEM((2, 2) + slab, BF16),
            pltpu.VMEM((2, CHUNK, CHUNK), BF16),
            pltpu.VMEM((CHUNK, WIDTH), BF16),
            pltpu.VMEM((TILES,) + slab, BF16),
            pltpu.VMEM((TILES,) + slab, BF16),
            pltpu.VMEM((2, 8) + bits, F32),
            pltpu.VMEM((2, 8) + bits, BF16),
            pltpu.VMEM((2, 8) + bits, BF16),
            pltpu.VMEM((2, 8) + bits, BF16),
            pltpu.VMEM((2,) + bits, BF16),
            pltpu.VMEM((2,) + bits, BF16),
            pltpu.VMEM((2, 2) + bits, BF16),
            pltpu.VMEM((2, 2) + bits, BF16),
            pltpu.VMEM((2,) + bits, BF16),
            pltpu.VMEM((2,) + bits, BF16),
            pltpu.VMEM((2, CHUNK, WIDTH), F32),
            pltpu.VMEM((2, CHUNK, WIDTH), F32),
            pltpu.VMEM((CHUNK, WIDTH), F32),
            pltpu.VMEM((128, WIDTH), F32),
            pltpu.VMEM((3, 32, WIDTH), F32),
            pltpu.VMEM((3, 8, WIDTH), F32),
            pltpu.VMEM((3, 8, 128), F32),
            pltpu.SemaphoreType.DMA((WIRES,)),
            pltpu.SemaphoreType.DMA((WIRES,)),
        ],
        compiler_params=pltpu.CompilerParams(
            collective_id=0, has_side_effects=True, vmem_limit_bytes=62 * 1024 * 1024
        ),
    )(
        table,
        xt,
        tile_values.reshape(SLOTS, TILE, TILE),
        layer_weight.reshape(16, 2, 16, WIDTH),
        cotangent,
    )
    grad_features = gft.transpose(1, 3, 0, 2).reshape(TILES * TILE, 32)
    return hid, gw.reshape(WIDTH, WIDTH), grad_features


def solution(mesh):
    in_specs = (
        P("col", "row"),
        P(),
        P("row", "col", None, None, None),
        P("row", "col", None, None),
        P("row", "col"),
        P(("row", "col"), None),
    )
    out_specs = (P(("row", "col"), None), P(), P("col", "row"))
    return jax.shard_map(body, mesh=mesh, in_specs=in_specs, out_specs=out_specs, check_vma=False)
```

```python
import jax
import jax.numpy as jnp
from jax import lax
from jax.experimental import pallas as pl
from jax.experimental.pallas import tpu as pltpu
from jax.sharding import PartitionSpec as P

MESH = pl.DeviceIdType.MESH
BF16 = jnp.bfloat16
F32 = jnp.float32

SLOTS = 96
TILES = 32
TILE = 128
WIDTH = 512
CHUNK = 128
NODES = 256
UNROLL = 8
WIRES = 192

NT = (((1,), (1,)), ((), ()))
NN = (((1,), (0,)), ((), ()))
TN = (((0,), (0,)), ((), ()))


def dot(a, b, dims):
    return lax.dot_general(a, b, dims, preferred_element_type=F32)


def order_table(main, other, live):
    side = (TILE, TILE)
    lane = lax.broadcasted_iota(jnp.int32, (1, TILE), 1)
    lanes = lax.broadcasted_iota(jnp.int32, side, 1)
    key = jnp.where(live, main * 64 + other, 4096 + lane)
    across = jnp.broadcast_to(key, side)
    down = across.T
    before = down < across
    rank = jnp.sum(before.astype(jnp.int32), axis=0, keepdims=True)
    same = jnp.where(before & ((down >> 6) == (across >> 6)), 1, 0)
    opens = jnp.where(jnp.sum(same, axis=0, keepdims=True) > 0, 0, 1)
    fact = lane + 128 * jnp.where(live, other, 0) + 4096 * opens
    places = jnp.broadcast_to(rank, side).T == lanes
    facts = jnp.sum(jnp.where(places, jnp.broadcast_to(fact, side).T, 0), axis=0, keepdims=True)
    upto = jnp.sum(((down >> 6) <= lanes).astype(jnp.int32), axis=0, keepdims=True)
    count = jnp.sum(((down >> 6) == lanes).astype(jnp.int32), axis=0, keepdims=True)
    return [facts & 127, (facts >> 7) & 31, facts >> 12, jnp.maximum(upto - 1, 0), count]


def kernel(
    count, coords, xin, tiles_hbm, weight_hbm, cot_hbm, hid, gw, gft,
    xg0, xg1, xg2, xg3, run, ys, yown, xrl, xrr, xinl, xinr, zs, zrl, zrr, zinl, zinr,
    aggt, gpre, gg0, gg1, gg2, gg3, bown, bsend, cin, yb, yrl, yrr, yinl, yinr, zout, zpin,
    gsum, gout, rin_c, rin_z, rin_y, rin_x, rin_h, tiles, weight, cot, drawn, made, table,
    send_sem, recv_sem, local_sem,
):
    xg, gg = (xg0, xg1, xg2, xg3), (gg0, gg1, gg2, gg3)
    r = lax.axis_index("row")
    c = lax.axis_index("col")
    y, zl, core = r // 4, (r // 2) % 2, r % 2
    x, zh = c // 4, c % 4

    def turn(v, by):
        return (v + by) % 4

    def at_y(by):
        return (turn(y, by) * 4 + r % 4, c)

    def at_x(by):
        return (r, turn(x, by) * 4 + zh)

    def at_h(by):
        return (r, x * 4 + turn(zh, by))

    at_z = (r + 2 - 4 * zl, c)
    at_core = (r + 1 - 2 * core, c)

    barrier = pltpu.get_barrier_semaphore()
    peers = [at_z, at_core] + [f(by) for f in (at_y, at_x, at_h) for by in (1, 2, 3)]
    for peer in peers:
        pl.semaphore_signal(barrier, inc=1, device_id=peer, device_id_type=MESH)
    moves = [
        pltpu.make_async_copy(src, dst, local_sem.at[i])
        for i, (src, dst) in enumerate(((tiles_hbm, tiles), (weight_hbm, weight), (cot_hbm, cot)))
    ]
    for move in moves:
        move.start()

    def loop(n, f):
        def step(i, carry):
            f(i)
            return carry

        lax.fori_loop(0, n, step, 0)

    place = 2 * y + zl
    place_z = 2 * y + 1 - zl

    def laid_out(s):
        cut = pl.ds(pl.multiple_of(s * TILE, TILE), TILE)
        for k in range(2):
            xg[2 * k][place, s] = xin[16 * k : 16 * k + 16, cut]

    loop(TILES, laid_out)
    pl.semaphore_wait(barrier, len(peers))

    started = []

    def send(src, dst, peer):
        i = len(started)
        copy = pltpu.make_async_remote_copy(
            src_ref=src, dst_ref=dst, send_sem=send_sem.at[i], recv_sem=recv_sem.at[i],
            device_id=peer, device_id_type=MESH,
        )
        copy.start()
        started.append(copy)
        return copy

    def gather_row(k):
        own, across = xg[2 * k], xg[2 * k + 1]

        def part(owner, h):
            return own.at[owner, pl.ds(16 * h, 16)]

        inside = []

        def pass_on(owner):
            inside.append(send(own.at[owner], across.at[owner], at_core))

        to_z = send(own.at[place], own.at[place], at_z)
        up = send(own.at[place], own.at[place], at_y(1))
        down = send(own.at[place], own.at[place], at_y(3))
        pass_on(place)
        yield
        to_z.wait_recv()
        up_z = send(own.at[place_z], own.at[place_z], at_y(1))
        down_z = send(own.at[place_z], own.at[place_z], at_y(3))
        pass_on(place_z)
        yield
        relays = []
        for copy, by, side in ((up, 3, zl), (down, 1, zl), (up_z, 3, 1 - zl), (down_z, 1, 1 - zl)):
            owner = 2 * turn(y, by) + side
            copy.wait_recv()
            if by == 3:
                relays.append(send(part(owner, 0), part(owner, 0), at_y(1)))
            else:
                relays.append(send(part(owner, 1), part(owner, 1), at_y(3)))
            pass_on(owner)
        yield
        for side, pair in ((zl, relays[:2]), (1 - zl, relays[2:])):
            for copy in pair:
                copy.wait_recv()
            pass_on(2 * turn(y, 2) + side)
        yield
        for copy in inside:
            copy.wait_recv()
        yield

    def sweep(load, dims, base):
        def step(u, total):
            for v in range(UNROLL):
                t = u * UNROLL + v
                block = tiles[table[base, t]]
                product = dot(load(table[base + 1, t]), block, dims)
                total = jnp.where(table[base + 2, t] > 0, product, total + product)
                run[t] = total
            return total

        lax.fori_loop(0, SLOTS // UNROLL, step, jnp.zeros((CHUNK, TILE), F32))

    def segment(base, d):
        return jnp.where(table[base + 4, d] > 0, run[table[base + 3, d]], 0.0)

    def reduce_col(k):
        sweep(lambda s: xg[k][:, s].reshape(CHUNK, TILE), NT, 0)
        yield
        far, nxt, prv, own = (8 * turn(x, by) for by in (2, 1, 3, 0))

        def rounded(base):
            def one(i):
                ys[k, base + i] = segment(0, base + i).astype(BF16)

            loop(8, one)

        rounded(far)
        relay_l = send(ys.at[k, pl.ds(far, 4)], xrl.at[k], at_x(1))
        relay_r = send(ys.at[k, pl.ds(far + 4, 4)], xrr.at[k], at_x(3))
        rounded(nxt)
        plain_l = send(ys.at[k, pl.ds(nxt + 4, 4)], xinl.at[k, pl.ds(4, 4)], at_x(1))
        rounded(prv)
        plain_r = send(ys.at[k, pl.ds(prv, 4)], xinr.at[k, pl.ds(0, 4)], at_x(3))

        def kept(i):
            yown[k, i] = segment(0, own + i)

        loop(8, kept)
        yield

        def passed_l(i):
            ys[k, nxt + i] = (ys[k, nxt + i].astype(F32) + xrl[k, i].astype(F32)).astype(BF16)

        def passed_r(i):
            ys[k, prv + 4 + i] = (ys[k, prv + 4 + i].astype(F32) + xrr[k, i].astype(F32)).astype(BF16)

        relay_l.wait_recv()
        loop(4, passed_l)
        sum_l = send(ys.at[k, pl.ds(nxt, 4)], xinl.at[k, pl.ds(0, 4)], at_x(1))
        relay_r.wait_recv()
        loop(4, passed_r)
        sum_r = send(ys.at[k, pl.ds(prv + 4, 4)], xinr.at[k, pl.ds(4, 4)], at_x(3))
        yield
        for copy in (plain_l, plain_r, sum_l, sum_r):
            copy.wait_recv()

        def summed(i):
            total = yown[k, i] + xinl[k, i].astype(F32) + xinr[k, i].astype(F32)
            yown[k, i] = total
            zs[k, i] = total.astype(BF16)

        loop(8, summed)
        far, nxt, prv, own = (2 * turn(zh, by) for by in (2, 1, 3, 0))
        relay_l = send(zs.at[k, far], zrl.at[k], at_h(1))
        relay_r = send(zs.at[k, far + 1], zrr.at[k], at_h(3))
        plain_l = send(zs.at[k, nxt + 1], zinl.at[k, 1], at_h(1))
        plain_r = send(zs.at[k, prv], zinr.at[k, 0], at_h(3))
        yield
        relay_l.wait_recv()
        zs[k, nxt] = (yown[k, nxt] + zrl[k].astype(F32)).astype(BF16)
        sum_l = send(zs.at[k, nxt], zinl.at[k, 0], at_h(1))
        relay_r.wait_recv()
        zs[k, prv + 1] = (yown[k, prv + 1] + zrr[k].astype(F32)).astype(BF16)
        sum_r = send(zs.at[k, prv + 1], zinr.at[k, 1], at_h(3))
        yield
        for copy in (plain_l, plain_r, sum_l, sum_r):
            copy.wait_recv()
        for i in range(2):
            total = yown[k, own + i] + zinl[k, i].astype(F32) + zinr[k, i].astype(F32)
            aggt[k, :, i * TILE : (i + 1) * TILE] = total.astype(BF16)
        yield

    def gather_col(k):
        def whole(by_x, by_h):
            return gg[k].at[pl.ds(2 * (turn(x, by_x) * 4 + turn(zh, by_h)), 2)]

        def half(by_h, i):
            return gg[k].at[2 * (x * 4 + turn(zh, by_h)) + i]

        right, left = {}, {}

        def along_x(by_h):
            right[by_h] = send(whole(0, by_h), whole(0, by_h), at_x(1))
            left[by_h] = send(whole(0, by_h), whole(0, by_h), at_x(3))

        up = send(whole(0, 0), whole(0, 0), at_h(1))
        down = send(whole(0, 0), whole(0, 0), at_h(3))
        yield
        along_x(0)
        yield
        up.wait_recv()
        relay_up = send(half(3, 0), half(3, 0), at_h(1))
        along_x(3)
        down.wait_recv()
        relay_down = send(half(1, 1), half(1, 1), at_h(3))
        along_x(1)
        yield
        relay_up.wait_recv()
        relay_down.wait_recv()
        along_x(2)
        yield
        relays = []
        for by_h in (0, 3, 1, 2):
            right[by_h].wait_recv()
            if by_h in (0, 1):
                relays.append(send(whole(3, by_h), whole(3, by_h), at_x(1)))
            left[by_h].wait_recv()
            if by_h in (2, 3):
                relays.append(send(whole(1, by_h), whole(1, by_h), at_x(3)))
        yield
        for copy in relays:
            copy.wait_recv()
        yield

    def reduce_row(k):
        sweep(lambda d: gg[2 * k + 1][d], NN, 5)

        def leaving_core(s):
            bsend[k, :, s] = segment(5, s).reshape(8, 16, TILE).astype(BF16)

        loop(TILES, leaving_core)
        far, nxt, prv, own = (2 * turn(y, by) for by in (2, 1, 3, 0))
        inside = [send(bsend.at[k, pl.ds(b, 2)], cin.at[k, pl.ds(b, 2)], at_core) for b in (far, nxt, prv, own)]
        yield
        sweep(lambda d: gg[2 * k][d], NN, 5)

        def staying(s):
            bown[k, :, s] = segment(5, s).reshape(8, 16, TILE)

        loop(TILES, staying)

        def joined(base):
            for i in range(2):
                def rows(h):
                    cut = pl.ds(h * 8, 8)
                    total = bown[k, base + i, cut] + cin[k, base + i, cut].astype(F32)
                    bown[k, base + i, cut] = total
                    yb[k, base + i, cut] = total.astype(BF16)

                loop(4, rows)

        inside[0].wait_recv()
        joined(far)
        relay_l = send(yb.at[k, far], yrl.at[k], at_y(1))
        relay_r = send(yb.at[k, far + 1], yrr.at[k], at_y(3))
        inside[1].wait_recv()
        joined(nxt)
        plain_l = send(yb.at[k, nxt + 1], yinl.at[k, 1], at_y(1))
        inside[2].wait_recv()
        joined(prv)
        plain_r = send(yb.at[k, prv], yinr.at[k, 0], at_y(3))
        inside[3].wait_recv()
        joined(own)
        yield

        def passed(at, came):
            def rows(h):
                cut = pl.ds(h * 8, 8)
                yb[k, at, cut] = (bown[k, at, cut] + came[k, cut].astype(F32)).astype(BF16)

            loop(4, rows)

        relay_l.wait_recv()
        passed(nxt, yrl)
        sum_l = send(yb.at[k, nxt], yinl.at[k, 0], at_y(1))
        relay_r.wait_recv()
        passed(prv + 1, yrr)
        sum_r = send(yb.at[k, prv + 1], yinr.at[k, 1], at_y(3))
        yield
        for copy in (plain_l, plain_r, sum_l, sum_r):
            copy.wait_recv()

        def total_of(i, cut):
            return bown[k, own + i, cut] + yinl[k, i, cut].astype(F32) + yinr[k, i, cut].astype(F32)

        def leaving(h):
            cut = pl.ds(h * 8, 8)
            zout[k, cut] = total_of(1 - zl, cut).astype(BF16)

        loop(4, leaving)
        to_z = send(zout.at[k], zpin.at[k], at_z)
        yield
        to_z.wait_recv()

        def final(s):
            cut = pl.ds(pl.multiple_of(s * TILE, TILE), TILE)
            gft[16 * k : 16 * k + 16, cut] = (total_of(zl, s) + zpin[k, s].astype(F32)).astype(BF16)

        loop(TILES, final)
        yield

    def reduce_weight():
        rows_y = pl.multiple_of(32 * y, 32)
        rows_x = pl.multiple_of(rows_y + 8 * x, 8)
        lanes = pl.multiple_of(128 * zh, 128)
        copy = send(gsum.at[1 - core], rin_c, at_core)
        yield
        copy.wait_recv()
        gsum[core] += rin_c[...]
        copy = send(gsum.at[core, 1 - zl], rin_z, at_z)
        yield
        copy.wait_recv()
        gsum[core, zl] += rin_z[...]
        copies = [
            send(
                gsum.at[core, zl, pl.ds(pl.multiple_of(32 * turn(y, by), 32), 32)],
                rin_y.at[by - 1], at_y(by),
            )
            for by in (1, 2, 3)
        ]
        yield
        for copy in copies:
            copy.wait_recv()
        gsum[core, zl, pl.ds(rows_y, 32)] += rin_y[0] + rin_y[1] + rin_y[2]
        copies = [
            send(
                gsum.at[core, zl, pl.ds(pl.multiple_of(rows_y + 8 * turn(x, by), 8), 8)],
                rin_x.at[by - 1], at_x(by),
            )
            for by in (1, 2, 3)
        ]
        yield
        for copy in copies:
            copy.wait_recv()
        gsum[core, zl, pl.ds(rows_x, 8)] += rin_x[0] + rin_x[1] + rin_x[2]
        copies = [
            send(
                gsum.at[core, zl, pl.ds(rows_x, 8), pl.ds(pl.multiple_of(128 * turn(zh, by), 128), 128)],
                rin_h.at[by - 1], at_h(by),
            )
            for by in (1, 2, 3)
        ]
        yield
        for copy in copies:
            copy.wait_recv()
        corner = (core, zl, pl.ds(rows_x, 8), pl.ds(lanes, 128))
        gout[corner] = gsum[corner] + rin_h[0] + rin_h[1] + rin_h[2]
        for cut, where in (
            (corner, [at_h(by) for by in (1, 2, 3)]),
            ((core, zl, pl.ds(rows_x, 8)), [at_x(by) for by in (1, 2, 3)]),
            ((core, zl, pl.ds(rows_y, 32)), [at_y(by) for by in (1, 2, 3)]),
            ((core, zl), [at_z]),
            ((core,), [at_core]),
        ):
            copies = [send(gout.at[cut], gout.at[cut], peer) for peer in where]
            yield
            for copy in copies:
                copy.wait_recv()
        for h in range(2):
            for k in range(2):
                gw[:, h, k] = gout[h, k].reshape(8, 16, WIDTH)
        yield

    def go(gen, times=1):
        for _ in range(times):
            next(gen)

    rows = [gather_row(k) for k in range(2)]
    cols = [reduce_col(q) for q in range(4)]
    go(rows[0])
    drawn[...] = jnp.zeros((8, TILE), jnp.int32)
    drawn[0:2, 0:SLOTS] = coords[...]
    dest, source = drawn[0:1, :], drawn[1:2, :]
    live = lax.broadcasted_iota(jnp.int32, (1, TILE), 1) < count[0, 0]
    for i, row in enumerate(order_table(dest, source, live) + order_table(source, dest, live)):
        made[i : i + 1, :] = row
    to_table = pltpu.make_async_copy(made, table, local_sem.at[3])
    to_table.start()
    go(rows[0], 2)
    go(rows[1])
    to_table.wait()
    for move in moves:
        move.wait()
    go(rows[0])
    go(cols[0], 2)
    go(rows[1])
    go(rows[0])
    go(cols[1])
    go(cols[0])
    go(cols[1])
    go(rows[1], 2)
    go(cols[2])
    go(cols[1])
    go(cols[2])
    go(cols[0])
    go(rows[1])
    go(cols[3])
    go(cols[2])
    go(cols[3])
    go(cols[0])
    go(cols[1])
    go(cols[0])
    go(cols[3])
    go(cols[1])
    go(cols[2])
    go(cols[1])
    go(cols[2])
    go(cols[3])
    go(cols[2])
    go(cols[3], 2)

    def core_of(q):
        return core if q % 2 == 0 else 1 - core

    for n in range(2):
        cut = slice(n * NODES, (n + 1) * NODES)
        pre = jnp.zeros((NODES, NODES), F32)
        for q in range(4):
            pre += dot(aggt[q], weight[:, core_of(q), q // 2, :, cut].reshape(CHUNK, NODES), TN)
        low = jnp.exp(jnp.minimum(pre, 0.0))
        hid[:, cut] = jnp.where(pre > 0, pre, low - 1.0).astype(BF16)
        slope = jnp.where(pre > 0, 1.0, low)
        gpre[:, cut] = (cot[:, cut].astype(F32) * slope).astype(BF16)

    def grad_agg(q):
        part = dot(weight[:, core_of(q), q // 2].reshape(CHUNK, WIDTH), gpre[...], NT).astype(BF16)
        for i in range(2):
            gg[q][2 * c + i] = part[:, i * TILE : (i + 1) * TILE]

    a, b, d, e = 1, 0, 3, 2
    cols = [gather_col(q) for q in range(4)]
    rows = [reduce_row(k) for k in range(2)]
    total = reduce_weight()
    grad_agg(a)
    go(cols[a], 2)
    for q in (b, d, e):
        grad_agg(q)
    for q in range(4):
        gsum[core_of(q), q // 2] = dot(aggt[q], gpre[...], NN)
    go(cols[a])
    go(cols[b])
    go(total)
    go(cols[a])
    go(cols[b], 3)
    go(total)
    go(cols[a])
    go(cols[d], 3)
    go(total)
    go(cols[b])
    go(cols[d])
    go(total)
    go(cols[a])
    go(rows[0])
    go(cols[e], 3)
    go(cols[d])
    go(cols[e])
    go(total)
    go(cols[b])
    go(rows[0])
    go(total)
    go(cols[e])
    go(cols[d])
    go(rows[1])
    go(total)
    go(rows[0])
    go(total)
    go(cols[e])
    go(rows[1])
    go(total)
    go(rows[0])
    go(rows[1])
    go(total)
    go(rows[0])
    go(rows[1])
    go(total)
    go(rows[1])
    for copy in started:
        copy.wait_send()


def hand_over(*refs):
    sources, targets, sems = refs[:3], refs[3:6], refs[6]
    copies = [pltpu.make_async_copy(s, t, sems.at[i]) for i, (s, t) in enumerate(zip(sources, targets))]
    for copy in copies:
        copy.start()
    for copy in copies:
        copy.wait()


def body(node_features, layer_weight, tile_values, tile_coords, tile_count, cotangent):
    vmem = pl.BlockSpec(memory_space=pltpu.VMEM)
    smem = pl.BlockSpec(memory_space=pltpu.SMEM)
    hbm = pl.BlockSpec(memory_space=pl.ANY)
    slab = (CHUNK, TILE)
    bits = (TILES, 16, TILE)
    shapes = [
        jax.ShapeDtypeStruct((NODES, WIDTH), BF16),
        jax.ShapeDtypeStruct((8, 2, 2, 16, WIDTH), F32),
        jax.ShapeDtypeStruct((32, TILES * TILE), BF16),
    ]
    results = pl.pallas_call(
        kernel,
        out_shape=shapes,
        in_specs=[smem, vmem, vmem, hbm, hbm, hbm],
        out_specs=[vmem] * 3,
        scratch_shapes=[
            *[pltpu.VMEM((8,) + bits, BF16)] * 4,
            pltpu.VMEM((SLOTS,) + slab, F32),
            pltpu.VMEM((4, TILES) + slab, BF16),
            pltpu.VMEM((4, 8) + slab, F32),
            pltpu.VMEM((4, 4) + slab, BF16),
            pltpu.VMEM((4, 4) + slab, BF16),
            pltpu.VMEM((4, 8) + slab, BF16),
            pltpu.VMEM((4, 8) + slab, BF16),
            pltpu.VMEM((4, 8) + slab, BF16),
            pltpu.VMEM((4,) + slab, BF16),
            pltpu.VMEM((4,) + slab, BF16),
            pltpu.VMEM((4, 2) + slab, BF16),
            pltpu.VMEM((4, 2) + slab, BF16),
            pltpu.VMEM((4, CHUNK, NODES), BF16),
            pltpu.VMEM((NODES, WIDTH), BF16),
            *[pltpu.VMEM((TILES,) + slab, BF16)] * 4,
            pltpu.VMEM((2, 8) + bits, F32),
            pltpu.VMEM((2, 8) + bits, BF16),
            pltpu.VMEM((2, 8) + bits, BF16),
            pltpu.VMEM((2, 8) + bits, BF16),
            pltpu.VMEM((2,) + bits, BF16),
            pltpu.VMEM((2,) + bits, BF16),
            pltpu.VMEM((2, 2) + bits, BF16),
            pltpu.VMEM((2, 2) + bits, BF16),
            pltpu.VMEM((2,) + bits, BF16),
            pltpu.VMEM((2,) + bits, BF16),
            pltpu.VMEM((2, 2, 128, WIDTH), F32),
            pltpu.VMEM((2, 2, 128, WIDTH), F32),
            pltpu.VMEM((2, 128, WIDTH), F32),
            pltpu.VMEM((128, WIDTH), F32),
            pltpu.VMEM((3, 32, WIDTH), F32),
            pltpu.VMEM((3, 8, WIDTH), F32),
            pltpu.VMEM((3, 8, 128), F32),
            pltpu.VMEM((SLOTS, TILE, TILE), BF16),
            pltpu.VMEM((8, 2, 2, 16, WIDTH), BF16),
            pltpu.VMEM((NODES, WIDTH), BF16),
            pltpu.VMEM((8, TILE), jnp.int32),
            pltpu.VMEM((16, TILE), jnp.int32),
            pltpu.SMEM((16, TILE), jnp.int32),
            pltpu.SemaphoreType.DMA((WIRES,)),
            pltpu.SemaphoreType.DMA((WIRES,)),
            pltpu.SemaphoreType.DMA((4,)),
        ],
        compiler_params=pltpu.CompilerParams(
            collective_id=0, has_side_effects=True, vmem_limit_bytes=62 * 1024 * 1024
        ),
    )(
        tile_count,
        tile_coords.reshape(SLOTS, 2).T,
        node_features.T,
        tile_values.reshape(SLOTS, TILE, TILE),
        layer_weight.reshape(8, 2, 2, 16, WIDTH),
        cotangent,
    )
    hid, gw, gft = pl.pallas_call(
        hand_over,
        out_shape=shapes,
        in_specs=[vmem] * 3,
        out_specs=[hbm] * 3,
        scratch_shapes=[pltpu.SemaphoreType.DMA((3,))],
    )(*results)
    return hid, gw.reshape(WIDTH, WIDTH), gft.T


def solution(mesh):
    in_specs = (
        P("col", "row"),
        P(),
        P("row", "col", None, None, None),
        P("row", "col", None, None),
        P("row", "col"),
        P(("row", "col"), None),
    )
    out_specs = (P(("row", "col"), None), P(), P("col", "row"))
    return jax.shard_map(body, mesh=mesh, in_specs=in_specs, out_specs=out_specs, check_vma=False)
```

```python
import jax
import jax.numpy as jnp
from jax import lax
from jax.experimental import pallas as pl
from jax.experimental.pallas import tpu as pltpu
from jax.sharding import PartitionSpec as P

MESH = pl.DeviceIdType.MESH
BF16 = jnp.bfloat16
F32 = jnp.float32

SLOTS = 96
TILES = 32
TILE = 128
WIDTH = 512
CHUNK = 128
NODES = 256
UNROLL = 8
WIRES = 192

NT = (((1,), (1,)), ((), ()))
NN = (((1,), (0,)), ((), ()))
TN = (((0,), (0,)), ((), ()))


def dot(a, b, dims):
    return lax.dot_general(a, b, dims, preferred_element_type=F32)


def order_table(main, other, live):
    side = (TILE, TILE)
    lane = lax.broadcasted_iota(jnp.int32, (1, TILE), 1)
    lanes = lax.broadcasted_iota(jnp.int32, side, 1)
    key = jnp.where(live, main * 64 + other, 4096 + lane)
    across = jnp.broadcast_to(key, side)
    down = across.T
    before = down < across
    rank = jnp.sum(before.astype(jnp.int32), axis=0, keepdims=True)
    same = jnp.where(before & ((down >> 6) == (across >> 6)), 1, 0)
    opens = jnp.where(jnp.sum(same, axis=0, keepdims=True) > 0, 0, 1)
    fact = lane + 128 * jnp.where(live, other, 0) + 4096 * opens
    places = jnp.broadcast_to(rank, side).T == lanes
    facts = jnp.sum(jnp.where(places, jnp.broadcast_to(fact, side).T, 0), axis=0, keepdims=True)
    upto = jnp.sum(((down >> 6) <= lanes).astype(jnp.int32), axis=0, keepdims=True)
    count = jnp.sum(((down >> 6) == lanes).astype(jnp.int32), axis=0, keepdims=True)
    return [facts & 127, (facts >> 7) & 31, facts >> 12, jnp.maximum(upto - 1, 0), count]


def kernel(
    count, coords, xin, tiles_hbm, weight_hbm, cot_hbm, hid, gw, gft,
    xg0, xg1, xg2, xg3, run, ys, yown, xrl, xrr, xinl, xinr, zs, zrl, zrr, zinl, zinr,
    aggt, gpre, gg0, gg1, gg2, gg3, bown, bsend, cin, yb, yrl, yrr, yinl, yinr, zout, zpin,
    gsum, gout, rin_c, rin_z, rin_y, rin_x, rin_h, tiles, weight, cot, drawn, made, table,
    send_sem, recv_sem, local_sem,
):
    xg, gg = (xg0, xg1, xg2, xg3), (gg0, gg1, gg2, gg3)
    r = lax.axis_index("row")
    c = lax.axis_index("col")
    y, zl, core = r // 4, (r // 2) % 2, r % 2
    x, zh = c // 4, c % 4

    def turn(v, by):
        return (v + by) % 4

    def at_y(by):
        return (turn(y, by) * 4 + r % 4, c)

    def at_x(by):
        return (r, turn(x, by) * 4 + zh)

    def at_h(by):
        return (r, x * 4 + turn(zh, by))

    at_z = (r + 2 - 4 * zl, c)
    at_core = (r + 1 - 2 * core, c)

    barrier = pltpu.get_barrier_semaphore()
    peers = [at_z, at_core] + [f(by) for f in (at_y, at_x, at_h) for by in (1, 2, 3)]
    for peer in peers:
        pl.semaphore_signal(barrier, inc=1, device_id=peer, device_id_type=MESH)
    moves = [
        pltpu.make_async_copy(src, dst, local_sem.at[i])
        for i, (src, dst) in enumerate(((tiles_hbm, tiles), (weight_hbm, weight), (cot_hbm, cot)))
    ]
    for move in moves:
        move.start()

    def loop(n, f):
        def step(i, carry):
            f(i)
            return carry

        lax.fori_loop(0, n, step, 0)

    place = 2 * y + zl
    place_z = 2 * y + 1 - zl

    def laid_out(s):
        cut = pl.ds(pl.multiple_of(s * TILE, TILE), TILE)
        for k in range(2):
            xg[2 * k][place, s] = xin[16 * k : 16 * k + 16, cut]

    loop(TILES, laid_out)
    pl.semaphore_wait(barrier, len(peers))

    started = []

    def send(src, dst, peer):
        i = len(started)
        copy = pltpu.make_async_remote_copy(
            src_ref=src, dst_ref=dst, send_sem=send_sem.at[i], recv_sem=recv_sem.at[i],
            device_id=peer, device_id_type=MESH,
        )
        copy.start()
        started.append(copy)
        return copy

    def gather_row(k):
        own, across = xg[2 * k], xg[2 * k + 1]

        def part(owner, h):
            return own.at[owner, pl.ds(16 * h, 16)]

        inside = []

        def pass_on(owner):
            inside.append(send(own.at[owner], across.at[owner], at_core))

        to_z = send(own.at[place], own.at[place], at_z)
        up = send(own.at[place], own.at[place], at_y(1))
        down = send(own.at[place], own.at[place], at_y(3))
        pass_on(place)
        yield
        to_z.wait_recv()
        up_z = send(own.at[place_z], own.at[place_z], at_y(1))
        down_z = send(own.at[place_z], own.at[place_z], at_y(3))
        pass_on(place_z)
        yield
        relays = []
        for copy, by, side in ((up, 3, zl), (down, 1, zl), (up_z, 3, 1 - zl), (down_z, 1, 1 - zl)):
            owner = 2 * turn(y, by) + side
            copy.wait_recv()
            if by == 3:
                relays.append(send(part(owner, 0), part(owner, 0), at_y(1)))
            else:
                relays.append(send(part(owner, 1), part(owner, 1), at_y(3)))
            pass_on(owner)
        yield
        for side, pair in ((zl, relays[:2]), (1 - zl, relays[2:])):
            for copy in pair:
                copy.wait_recv()
            pass_on(2 * turn(y, 2) + side)
        yield
        for copy in inside:
            copy.wait_recv()
        yield

    def sweep(load, dims, base):
        def step(u, total):
            for v in range(UNROLL):
                t = u * UNROLL + v
                block = tiles[table[base, t]]
                product = dot(load(table[base + 1, t]), block, dims)
                total = jnp.where(table[base + 2, t] > 0, product, total + product)
                run[t] = total
            return total

        lax.fori_loop(0, SLOTS // UNROLL, step, jnp.zeros((CHUNK, TILE), F32))

    def segment(base, d):
        return jnp.where(table[base + 4, d] > 0, run[table[base + 3, d]], 0.0)

    def reduce_col(k, z_first):
        spot_a, spot_b = (zh, x) if z_first else (x, zh)
        at_a, at_b = (at_h, at_x) if z_first else (at_x, at_h)

        def tile_of(base, i):
            return (i // 2) * 8 + base // 4 + i % 2 if z_first else base + i

        sweep(lambda s: xg[k][:, s].reshape(CHUNK, TILE), NT, 0)
        yield
        far, nxt, prv, own = (8 * turn(spot_a, by) for by in (2, 1, 3, 0))

        def rounded(base):
            def one(i):
                ys[k, base + i] = segment(0, tile_of(base, i)).astype(BF16)

            loop(8, one)

        rounded(far)
        relay_l = send(ys.at[k, pl.ds(far, 4)], xrl.at[k], at_a(1))
        relay_r = send(ys.at[k, pl.ds(far + 4, 4)], xrr.at[k], at_a(3))
        rounded(nxt)
        plain_l = send(ys.at[k, pl.ds(nxt + 4, 4)], xinl.at[k, pl.ds(4, 4)], at_a(1))
        rounded(prv)
        plain_r = send(ys.at[k, pl.ds(prv, 4)], xinr.at[k, pl.ds(0, 4)], at_a(3))

        def kept(i):
            yown[k, i] = segment(0, tile_of(own, i))

        loop(8, kept)
        yield

        def passed_l(i):
            ys[k, nxt + i] = (ys[k, nxt + i].astype(F32) + xrl[k, i].astype(F32)).astype(BF16)

        def passed_r(i):
            ys[k, prv + 4 + i] = (ys[k, prv + 4 + i].astype(F32) + xrr[k, i].astype(F32)).astype(BF16)

        relay_l.wait_recv()
        loop(4, passed_l)
        sum_l = send(ys.at[k, pl.ds(nxt, 4)], xinl.at[k, pl.ds(0, 4)], at_a(1))
        relay_r.wait_recv()
        loop(4, passed_r)
        sum_r = send(ys.at[k, pl.ds(prv + 4, 4)], xinr.at[k, pl.ds(4, 4)], at_a(3))
        yield
        for copy in (plain_l, plain_r, sum_l, sum_r):
            copy.wait_recv()

        def summed(i):
            total = yown[k, i] + xinl[k, i].astype(F32) + xinr[k, i].astype(F32)
            yown[k, i] = total
            zs[k, i] = total.astype(BF16)

        loop(8, summed)
        far, nxt, prv, own = (2 * turn(spot_b, by) for by in (2, 1, 3, 0))
        relay_l = send(zs.at[k, far], zrl.at[k], at_b(1))
        relay_r = send(zs.at[k, far + 1], zrr.at[k], at_b(3))
        plain_l = send(zs.at[k, nxt + 1], zinl.at[k, 1], at_b(1))
        plain_r = send(zs.at[k, prv], zinr.at[k, 0], at_b(3))
        yield
        relay_l.wait_recv()
        zs[k, nxt] = (yown[k, nxt] + zrl[k].astype(F32)).astype(BF16)
        sum_l = send(zs.at[k, nxt], zinl.at[k, 0], at_b(1))
        relay_r.wait_recv()
        zs[k, prv + 1] = (yown[k, prv + 1] + zrr[k].astype(F32)).astype(BF16)
        sum_r = send(zs.at[k, prv + 1], zinr.at[k, 1], at_b(3))
        yield
        for copy in (plain_l, plain_r, sum_l, sum_r):
            copy.wait_recv()
        for i in range(2):
            total = yown[k, own + i] + zinl[k, i].astype(F32) + zinr[k, i].astype(F32)
            aggt[k, :, i * TILE : (i + 1) * TILE] = total.astype(BF16)
        yield

    def gather_col(k, x_first):
        at_a, at_b = (at_x, at_h) if x_first else (at_h, at_x)

        def first_tile(by_a, by_b):
            by_x, by_h = (by_a, by_b) if x_first else (by_b, by_a)
            return 2 * (turn(x, by_x) * 4 + turn(zh, by_h))

        def whole(by_a, by_b):
            return gg[k].at[pl.ds(first_tile(by_a, by_b), 2)]

        def half(by_a, i):
            return gg[k].at[first_tile(by_a, 0) + i]

        right, left = {}, {}

        def along_b(by_a):
            right[by_a] = send(whole(by_a, 0), whole(by_a, 0), at_b(1))
            left[by_a] = send(whole(by_a, 0), whole(by_a, 0), at_b(3))

        up = send(whole(0, 0), whole(0, 0), at_a(1))
        down = send(whole(0, 0), whole(0, 0), at_a(3))
        yield
        along_b(0)
        yield
        up.wait_recv()
        relay_up = send(half(3, 0), half(3, 0), at_a(1))
        along_b(3)
        down.wait_recv()
        relay_down = send(half(1, 1), half(1, 1), at_a(3))
        along_b(1)
        yield
        relay_up.wait_recv()
        relay_down.wait_recv()
        along_b(2)
        yield
        relays = []
        for by_a in (0, 3, 1, 2):
            right[by_a].wait_recv()
            if by_a in (0, 1):
                relays.append(send(whole(by_a, 3), whole(by_a, 3), at_b(1)))
            left[by_a].wait_recv()
            if by_a in (2, 3):
                relays.append(send(whole(by_a, 1), whole(by_a, 1), at_b(3)))
        yield
        for copy in relays:
            copy.wait_recv()
        yield

    def reduce_row(k):
        sweep(lambda d: gg[2 * k + 1][d], NN, 5)

        def leaving_core(s):
            bsend[k, :, s] = segment(5, s).reshape(8, 16, TILE).astype(BF16)

        loop(TILES, leaving_core)
        far, nxt, prv, own = (2 * turn(y, by) for by in (2, 1, 3, 0))
        inside = [send(bsend.at[k, pl.ds(b, 2)], cin.at[k, pl.ds(b, 2)], at_core) for b in (far, nxt, prv, own)]
        yield
        sweep(lambda d: gg[2 * k][d], NN, 5)

        def staying(s):
            bown[k, :, s] = segment(5, s).reshape(8, 16, TILE)

        loop(TILES, staying)

        def joined(base):
            for i in range(2):
                def rows(h):
                    cut = pl.ds(h * 8, 8)
                    total = bown[k, base + i, cut] + cin[k, base + i, cut].astype(F32)
                    bown[k, base + i, cut] = total
                    yb[k, base + i, cut] = total.astype(BF16)

                loop(4, rows)

        inside[0].wait_recv()
        joined(far)
        relay_l = send(yb.at[k, far], yrl.at[k], at_y(1))
        relay_r = send(yb.at[k, far + 1], yrr.at[k], at_y(3))
        inside[1].wait_recv()
        joined(nxt)
        plain_l = send(yb.at[k, nxt + 1], yinl.at[k, 1], at_y(1))
        inside[2].wait_recv()
        joined(prv)
        plain_r = send(yb.at[k, prv], yinr.at[k, 0], at_y(3))
        inside[3].wait_recv()
        joined(own)
        yield

        def passed(at, came):
            def rows(h):
                cut = pl.ds(h * 8, 8)
                yb[k, at, cut] = (bown[k, at, cut] + came[k, cut].astype(F32)).astype(BF16)

            loop(4, rows)

        relay_l.wait_recv()
        passed(nxt, yrl)
        sum_l = send(yb.at[k, nxt], yinl.at[k, 0], at_y(1))
        relay_r.wait_recv()
        passed(prv + 1, yrr)
        sum_r = send(yb.at[k, prv + 1], yinr.at[k, 1], at_y(3))
        yield
        for copy in (plain_l, plain_r, sum_l, sum_r):
            copy.wait_recv()

        def total_of(i, cut):
            return bown[k, own + i, cut] + yinl[k, i, cut].astype(F32) + yinr[k, i, cut].astype(F32)

        def leaving(h):
            cut = pl.ds(h * 8, 8)
            zout[k, cut] = total_of(1 - zl, cut).astype(BF16)

        loop(4, leaving)
        to_z = send(zout.at[k], zpin.at[k], at_z)
        yield
        to_z.wait_recv()

        def final(s):
            cut = pl.ds(pl.multiple_of(s * TILE, TILE), TILE)
            gft[16 * k : 16 * k + 16, cut] = (total_of(zl, s) + zpin[k, s].astype(F32)).astype(BF16)

        loop(TILES, final)
        yield

    def reduce_weight():
        rows_y = pl.multiple_of(64 * (y % 2), 64)
        half_y = y // 2
        rows_z = pl.multiple_of(rows_y + 32 * zl, 32)
        rows_x = pl.multiple_of(rows_z + 8 * x, 8)
        lanes = pl.multiple_of(128 * zh, 128)

        def y_part(buffer, by):
            there = turn(y, by)
            return buffer.at[core, there // 2, pl.ds(pl.multiple_of(64 * (there % 2), 64), 64)]

        copy = send(gsum.at[1 - core], rin_c, at_core)
        yield
        copy.wait_recv()
        gsum[core] += rin_c[...]
        copies = [send(y_part(gsum, by), rin_y.at[by - 1], at_y(by)) for by in (1, 2, 3)]
        yield
        for copy in copies:
            copy.wait_recv()
        gsum[core, half_y, pl.ds(rows_y, 64)] += rin_y[0] + rin_y[1] + rin_y[2]
        across_z = pl.ds(pl.multiple_of(rows_y + 32 - 32 * zl, 32), 32)
        copy = send(gsum.at[core, half_y, across_z], rin_z, at_z)
        yield
        copy.wait_recv()
        gsum[core, half_y, pl.ds(rows_z, 32)] += rin_z[...]
        copies = [
            send(
                gsum.at[core, half_y, pl.ds(pl.multiple_of(rows_z + 8 * turn(x, by), 8), 8)],
                rin_x.at[by - 1], at_x(by),
            )
            for by in (1, 2, 3)
        ]
        yield
        for copy in copies:
            copy.wait_recv()
        gsum[core, half_y, pl.ds(rows_x, 8)] += rin_x[0] + rin_x[1] + rin_x[2]
        copies = [
            send(
                gsum.at[core, half_y, pl.ds(rows_x, 8), pl.ds(pl.multiple_of(128 * turn(zh, by), 128), 128)],
                rin_h.at[by - 1], at_h(by),
            )
            for by in (1, 2, 3)
        ]
        yield
        for copy in copies:
            copy.wait_recv()
        corner = (core, half_y, pl.ds(rows_x, 8), pl.ds(lanes, 128))
        gout[corner] = gsum[corner] + rin_h[0] + rin_h[1] + rin_h[2]
        for cut, where in (
            (corner, [at_h(by) for by in (1, 2, 3)]),
            ((core, half_y, pl.ds(rows_x, 8)), [at_x(by) for by in (1, 2, 3)]),
            ((core, half_y, pl.ds(rows_z, 32)), [at_z]),
            ((core, half_y, pl.ds(rows_y, 64)), [at_y(by) for by in (1, 2, 3)]),
            ((core,), [at_core]),
        ):
            copies = [send(gout.at[cut], gout.at[cut], peer) for peer in where]
            yield
            for copy in copies:
                copy.wait_recv()
        for h in range(2):
            for k in range(2):
                gw[:, h, k] = gout[h, k].reshape(8, 16, WIDTH)
        yield

    def go(gen, times=1):
        for _ in range(times):
            next(gen)

    rows = [gather_row(k) for k in range(2)]
    cols = [reduce_col(q, q == 1) for q in range(4)]
    go(rows[0])
    drawn[...] = jnp.zeros((8, TILE), jnp.int32)
    drawn[0:2, 0:SLOTS] = coords[...]
    dest, source = drawn[0:1, :], drawn[1:2, :]
    live = lax.broadcasted_iota(jnp.int32, (1, TILE), 1) < count[0, 0]
    for i, row in enumerate(order_table(dest, source, live) + order_table(source, dest, live)):
        made[i : i + 1, :] = row
    to_table = pltpu.make_async_copy(made, table, local_sem.at[3])
    to_table.start()
    go(rows[0], 2)
    go(rows[1])
    to_table.wait()
    for move in moves:
        move.wait()
    go(rows[0])
    go(cols[0], 2)
    go(rows[1])
    go(rows[0])
    go(cols[1], 2)
    go(rows[1])
    go(cols[0])
    go(rows[1])
    go(cols[2], 2)
    go(cols[0])
    go(rows[1])
    go(cols[3], 2)
    go(cols[2])
    go(cols[1])
    go(cols[0])
    go(cols[2])
    go(cols[3])
    go(cols[0])
    go(cols[1])
    go(cols[2])
    go(cols[3])
    go(cols[1])
    go(cols[2])
    go(cols[3])
    go(cols[1])
    go(cols[3])

    def core_of(q):
        return core if q % 2 == 0 else 1 - core

    for n in range(2):
        cut = slice(n * NODES, (n + 1) * NODES)
        pre = jnp.zeros((NODES, NODES), F32)
        for q in range(4):
            pre += dot(aggt[q], weight[:, core_of(q), q // 2, :, cut].reshape(CHUNK, NODES), TN)
        low = jnp.exp(jnp.minimum(pre, 0.0))
        hid[:, cut] = jnp.where(pre > 0, pre, low - 1.0).astype(BF16)
        slope = jnp.where(pre > 0, 1.0, low)
        gpre[:, cut] = (cot[:, cut].astype(F32) * slope).astype(BF16)

    def grad_agg(q):
        part = dot(weight[:, core_of(q), q // 2].reshape(CHUNK, WIDTH), gpre[...], NT).astype(BF16)
        for i in range(2):
            gg[q][2 * c + i] = part[:, i * TILE : (i + 1) * TILE]

    a, b, d, e = 1, 0, 3, 2
    cols = [gather_col(q, False) for q in range(4)]
    rows = [reduce_row(k) for k in range(2)]
    total = reduce_weight()
    grad_agg(a)
    go(cols[a], 2)
    for q in (b, d, e):
        grad_agg(q)
    for q in range(4):
        gsum[core_of(q), q // 2] = dot(aggt[q], gpre[...], NN)
    go(cols[a])
    go(cols[b])
    go(total)
    go(cols[a])
    go(cols[b], 3)
    go(total)
    go(cols[a])
    go(cols[d], 3)
    go(total)
    go(cols[b])
    go(cols[d])
    go(total)
    go(cols[a])
    go(rows[0])
    go(cols[e], 3)
    go(cols[d])
    go(cols[e])
    go(total)
    go(cols[b])
    go(rows[0])
    go(total)
    go(cols[e])
    go(cols[d])
    go(rows[1])
    go(total)
    go(rows[0])
    go(total)
    go(cols[e])
    go(rows[1])
    go(total)
    go(rows[0])
    go(rows[1])
    go(total)
    go(rows[0])
    go(rows[1])
    go(total)
    go(rows[1])
    for copy in started:
        copy.wait_send()


def hand_over(*refs):
    sources, targets, sems = refs[:3], refs[3:6], refs[6]
    copies = [pltpu.make_async_copy(s, t, sems.at[i]) for i, (s, t) in enumerate(zip(sources, targets))]
    for copy in copies:
        copy.start()
    for copy in copies:
        copy.wait()


def body(node_features, layer_weight, tile_values, tile_coords, tile_count, cotangent):
    vmem = pl.BlockSpec(memory_space=pltpu.VMEM)
    smem = pl.BlockSpec(memory_space=pltpu.SMEM)
    hbm = pl.BlockSpec(memory_space=pl.ANY)
    slab = (CHUNK, TILE)
    bits = (TILES, 16, TILE)
    shapes = [
        jax.ShapeDtypeStruct((NODES, WIDTH), BF16),
        jax.ShapeDtypeStruct((8, 2, 2, 16, WIDTH), F32),
        jax.ShapeDtypeStruct((32, TILES * TILE), BF16),
    ]
    results = pl.pallas_call(
        kernel,
        out_shape=shapes,
        in_specs=[smem, vmem, vmem, hbm, hbm, hbm],
        out_specs=[vmem] * 3,
        scratch_shapes=[
            *[pltpu.VMEM((8,) + bits, BF16)] * 4,
            pltpu.VMEM((SLOTS,) + slab, F32),
            pltpu.VMEM((4, TILES) + slab, BF16),
            pltpu.VMEM((4, 8) + slab, F32),
            pltpu.VMEM((4, 4) + slab, BF16),
            pltpu.VMEM((4, 4) + slab, BF16),
            pltpu.VMEM((4, 8) + slab, BF16),
            pltpu.VMEM((4, 8) + slab, BF16),
            pltpu.VMEM((4, 8) + slab, BF16),
            pltpu.VMEM((4,) + slab, BF16),
            pltpu.VMEM((4,) + slab, BF16),
            pltpu.VMEM((4, 2) + slab, BF16),
            pltpu.VMEM((4, 2) + slab, BF16),
            pltpu.VMEM((4, CHUNK, NODES), BF16),
            pltpu.VMEM((NODES, WIDTH), BF16),
            *[pltpu.VMEM((TILES,) + slab, BF16)] * 4,
            pltpu.VMEM((2, 8) + bits, F32),
            pltpu.VMEM((2, 8) + bits, BF16),
            pltpu.VMEM((2, 8) + bits, BF16),
            pltpu.VMEM((2, 8) + bits, BF16),
            pltpu.VMEM((2,) + bits, BF16),
            pltpu.VMEM((2,) + bits, BF16),
            pltpu.VMEM((2, 2) + bits, BF16),
            pltpu.VMEM((2, 2) + bits, BF16),
            pltpu.VMEM((2,) + bits, BF16),
            pltpu.VMEM((2,) + bits, BF16),
            pltpu.VMEM((2, 2, 128, WIDTH), F32),
            pltpu.VMEM((2, 2, 128, WIDTH), F32),
            pltpu.VMEM((2, 128, WIDTH), F32),
            pltpu.VMEM((32, WIDTH), F32),
            pltpu.VMEM((3, 64, WIDTH), F32),
            pltpu.VMEM((3, 8, WIDTH), F32),
            pltpu.VMEM((3, 8, 128), F32),
            pltpu.VMEM((SLOTS, TILE, TILE), BF16),
            pltpu.VMEM((8, 2, 2, 16, WIDTH), BF16),
            pltpu.VMEM((NODES, WIDTH), BF16),
            pltpu.VMEM((8, TILE), jnp.int32),
            pltpu.VMEM((16, TILE), jnp.int32),
            pltpu.SMEM((16, TILE), jnp.int32),
            pltpu.SemaphoreType.DMA((WIRES,)),
            pltpu.SemaphoreType.DMA((WIRES,)),
            pltpu.SemaphoreType.DMA((4,)),
        ],
        compiler_params=pltpu.CompilerParams(
            collective_id=0, has_side_effects=True, vmem_limit_bytes=62 * 1024 * 1024
        ),
    )(
        tile_count,
        tile_coords.reshape(SLOTS, 2).T,
        node_features.T,
        tile_values.reshape(SLOTS, TILE, TILE),
        layer_weight.reshape(8, 2, 2, 16, WIDTH),
        cotangent,
    )
    hid, gw, gft = pl.pallas_call(
        hand_over,
        out_shape=shapes,
        in_specs=[vmem] * 3,
        out_specs=[hbm] * 3,
        scratch_shapes=[pltpu.SemaphoreType.DMA((3,))],
    )(*results)
    return hid, gw.reshape(WIDTH, WIDTH), gft.T


def solution(mesh):
    in_specs = (
        P("col", "row"),
        P(),
        P("row", "col", None, None, None),
        P("row", "col", None, None),
        P("row", "col"),
        P(("row", "col"), None),
    )
    out_specs = (P(("row", "col"), None), P(), P("col", "row"))
    return jax.shard_map(body, mesh=mesh, in_specs=in_specs, out_specs=out_specs, check_vma=False)
```

```python
import jax
import jax.numpy as jnp
from jax import lax
from jax.experimental import pallas as pl
from jax.experimental.pallas import tpu as pltpu
from jax.sharding import PartitionSpec as P

MESH = pl.DeviceIdType.MESH
BF16 = jnp.bfloat16
F32 = jnp.float32

SLOTS = 96
TILES = 32
TILE = 128
WIDTH = 512
CHUNK = 128
NODES = 256
UNROLL = 8
WIRES = 208

NT = (((1,), (1,)), ((), ()))
NN = (((1,), (0,)), ((), ()))
TN = (((0,), (0,)), ((), ()))


def dot(a, b, dims):
    return lax.dot_general(a, b, dims, preferred_element_type=F32)


def order_table(main, other, live):
    side = (TILE, TILE)
    lane = lax.broadcasted_iota(jnp.int32, (1, TILE), 1)
    lanes = lax.broadcasted_iota(jnp.int32, side, 1)
    key = jnp.where(live, main * 64 + other, 4096 + lane)
    across = jnp.broadcast_to(key, side)
    down = across.T
    before = down < across
    rank = jnp.sum(before.astype(jnp.int32), axis=0, keepdims=True)
    same = jnp.where(before & ((down >> 6) == (across >> 6)), 1, 0)
    opens = jnp.where(jnp.sum(same, axis=0, keepdims=True) > 0, 0, 1)
    fact = lane + 128 * jnp.where(live, other, 0) + 4096 * opens
    places = jnp.broadcast_to(rank, side).T == lanes
    facts = jnp.sum(jnp.where(places, jnp.broadcast_to(fact, side).T, 0), axis=0, keepdims=True)
    upto = jnp.sum(((down >> 6) <= lanes).astype(jnp.int32), axis=0, keepdims=True)
    count = jnp.sum(((down >> 6) == lanes).astype(jnp.int32), axis=0, keepdims=True)
    return [facts & 127, (facts >> 7) & 31, facts >> 12, jnp.maximum(upto - 1, 0), count]


def kernel(
    count, coords, xin, tiles_hbm, weight_hbm, cot_hbm, hid, gw, gft,
    xg0, xg1, xg2, xg3, run, ys, yown, xrl, xrr, xinl, xinr, zs, zrl, zrr, zinl, zinr,
    aggt, acted, gpre, gg0, gg1, gg2, gg3, bown, bsend, cin, yb, yrl, yrr, yinl, yinr, zout, zpin,
    gsum, gout, rin_c, rin_z, rin_y, rin_x, rin_h, tiles, weight, cot, drawn, made, table,
    send_sem, recv_sem, local_sem,
):
    xg, gg = (xg0, xg1, xg2, xg3), (gg0, gg1, gg2, gg3)
    r = lax.axis_index("row")
    c = lax.axis_index("col")
    y, zl, core = r // 4, (r // 2) % 2, r % 2
    x, zh = c // 4, c % 4

    def turn(v, by):
        return (v + by) % 4

    def at_y(by):
        return (turn(y, by) * 4 + r % 4, c)

    def at_x(by):
        return (r, turn(x, by) * 4 + zh)

    def at_h(by):
        return (r, x * 4 + turn(zh, by))

    at_z = (r + 2 - 4 * zl, c)
    at_core = (r + 1 - 2 * core, c)

    barrier = pltpu.get_barrier_semaphore()
    peers = [at_z, at_core] + [f(by) for f in (at_y, at_x, at_h) for by in (1, 2, 3)]
    for peer in peers:
        pl.semaphore_signal(barrier, inc=1, device_id=peer, device_id_type=MESH)
    moves = [
        pltpu.make_async_copy(src, dst, local_sem.at[i])
        for i, (src, dst) in enumerate(((tiles_hbm, tiles), (weight_hbm, weight), (cot_hbm, cot)))
    ]
    for move in moves:
        move.start()

    def loop(n, f):
        def step(i, carry):
            f(i)
            return carry

        lax.fori_loop(0, n, step, 0)

    place = 2 * y + zl
    place_z = 2 * y + 1 - zl

    def laid_out(s):
        cut = pl.ds(pl.multiple_of(s * TILE, TILE), TILE)
        for k in range(2):
            xg[2 * k][place, s] = xin[16 * k : 16 * k + 16, cut]

    loop(TILES, laid_out)
    pl.semaphore_wait(barrier, len(peers))

    started = []

    def send(src, dst, peer):
        i = len(started)
        copy = pltpu.make_async_remote_copy(
            src_ref=src, dst_ref=dst, send_sem=send_sem.at[i], recv_sem=recv_sem.at[i],
            device_id=peer, device_id_type=MESH,
        )
        copy.start()
        started.append(copy)
        return copy

    def gather_row(k):
        own, across = xg[2 * k], xg[2 * k + 1]

        def part(owner, h):
            return own.at[owner, pl.ds(16 * h, 16)]

        inside = []

        def pass_on(owner):
            inside.append(send(own.at[owner], across.at[owner], at_core))

        def cross(owner, h, peer):
            return send(part(owner, h), part(owner, h), peer)

        to_z = [cross(place, h, at_z) for h in range(2)]
        up = [cross(place, 0, at_y(1)), None]
        down = [None, cross(place, 1, at_y(3))]
        up[1] = cross(place, 1, at_y(1))
        down[0] = cross(place, 0, at_y(3))
        pass_on(place)
        yield
        to_z[0].wait_recv()
        up_z = [cross(place_z, 0, at_y(1)), None]
        to_z[1].wait_recv()
        down_z = [None, cross(place_z, 1, at_y(3))]
        up_z[1] = cross(place_z, 1, at_y(1))
        down_z[0] = cross(place_z, 0, at_y(3))
        pass_on(place_z)
        yield
        relays = []
        for ups, downs, side in ((up, down, zl), (up_z, down_z, 1 - zl)):
            below, above = 2 * turn(y, 3) + side, 2 * turn(y, 1) + side
            ups[0].wait_recv()
            relays.append(cross(below, 0, at_y(1)))
            downs[1].wait_recv()
            relays.append(cross(above, 1, at_y(3)))
        for ups, downs, side in ((up, down, zl), (up_z, down_z, 1 - zl)):
            ups[1].wait_recv()
            pass_on(2 * turn(y, 3) + side)
            downs[0].wait_recv()
            pass_on(2 * turn(y, 1) + side)
        yield
        for side, pair in ((zl, relays[:2]), (1 - zl, relays[2:])):
            for copy in pair:
                copy.wait_recv()
            pass_on(2 * turn(y, 2) + side)
        yield
        for copy in inside:
            copy.wait_recv()
        yield

    def sweep(load, dims, base):
        def step(u, total):
            for v in range(UNROLL):
                t = u * UNROLL + v
                block = tiles[table[base, t]]
                product = dot(load(table[base + 1, t]), block, dims)
                total = jnp.where(table[base + 2, t] > 0, product, total + product)
                run[t] = total
            return total

        lax.fori_loop(0, SLOTS // UNROLL, step, jnp.zeros((CHUNK, TILE), F32))

    def segment(base, d):
        return jnp.where(table[base + 4, d] > 0, run[table[base + 3, d]], 0.0)

    def reduce_col(k, z_first):
        spot_a, spot_b = (zh, x) if z_first else (x, zh)
        at_a, at_b = (at_h, at_x) if z_first else (at_x, at_h)

        def tile_of(base, i):
            return (i // 2) * 8 + base // 4 + i % 2 if z_first else base + i

        sweep(lambda s: xg[k][:, s].reshape(CHUNK, TILE), NT, 0)
        yield
        far, nxt, prv, own = (8 * turn(spot_a, by) for by in (2, 1, 3, 0))

        def rounded(base):
            def one(i):
                ys[k, base + i] = segment(0, tile_of(base, i)).astype(BF16)

            loop(8, one)

        rounded(far)
        relay_l = send(ys.at[k, pl.ds(far, 4)], xrl.at[k], at_a(1))
        relay_r = send(ys.at[k, pl.ds(far + 4, 4)], xrr.at[k], at_a(3))
        rounded(nxt)
        plain_l = send(ys.at[k, pl.ds(nxt + 4, 4)], xinl.at[k, pl.ds(4, 4)], at_a(1))
        rounded(prv)
        plain_r = send(ys.at[k, pl.ds(prv, 4)], xinr.at[k, pl.ds(0, 4)], at_a(3))

        def kept(i):
            yown[k, i] = segment(0, tile_of(own, i))

        loop(8, kept)
        yield

        def passed_l(i):
            ys[k, nxt + i] = (ys[k, nxt + i].astype(F32) + xrl[k, i].astype(F32)).astype(BF16)

        def passed_r(i):
            ys[k, prv + 4 + i] = (ys[k, prv + 4 + i].astype(F32) + xrr[k, i].astype(F32)).astype(BF16)

        relay_l.wait_recv()
        loop(4, passed_l)
        sum_l = send(ys.at[k, pl.ds(nxt, 4)], xinl.at[k, pl.ds(0, 4)], at_a(1))
        relay_r.wait_recv()
        loop(4, passed_r)
        sum_r = send(ys.at[k, pl.ds(prv + 4, 4)], xinr.at[k, pl.ds(4, 4)], at_a(3))
        yield
        for copy in (plain_l, plain_r, sum_l, sum_r):
            copy.wait_recv()

        def summed(i):
            total = yown[k, i] + xinl[k, i].astype(F32) + xinr[k, i].astype(F32)
            yown[k, i] = total
            zs[k, i] = total.astype(BF16)

        loop(8, summed)
        far, nxt, prv, own = (2 * turn(spot_b, by) for by in (2, 1, 3, 0))
        relay_l = send(zs.at[k, far], zrl.at[k], at_b(1))
        relay_r = send(zs.at[k, far + 1], zrr.at[k], at_b(3))
        plain_l = send(zs.at[k, nxt + 1], zinl.at[k, 1], at_b(1))
        plain_r = send(zs.at[k, prv], zinr.at[k, 0], at_b(3))
        yield
        relay_l.wait_recv()
        zs[k, nxt] = (yown[k, nxt] + zrl[k].astype(F32)).astype(BF16)
        sum_l = send(zs.at[k, nxt], zinl.at[k, 0], at_b(1))
        relay_r.wait_recv()
        zs[k, prv + 1] = (yown[k, prv + 1] + zrr[k].astype(F32)).astype(BF16)
        sum_r = send(zs.at[k, prv + 1], zinr.at[k, 1], at_b(3))
        yield
        for copy in (plain_l, plain_r, sum_l, sum_r):
            copy.wait_recv()
        for i in range(2):
            total = yown[k, own + i] + zinl[k, i].astype(F32) + zinr[k, i].astype(F32)
            aggt[k, :, i * TILE : (i + 1) * TILE] = total.astype(BF16)
        yield

    def gather_col(k, x_first):
        at_a, at_b = (at_x, at_h) if x_first else (at_h, at_x)

        def first_tile(by_a, by_b):
            by_x, by_h = (by_a, by_b) if x_first else (by_b, by_a)
            return 2 * (turn(x, by_x) * 4 + turn(zh, by_h))

        def whole(by_a, by_b):
            return gg[k].at[pl.ds(first_tile(by_a, by_b), 2)]

        def half(by_a, i):
            return gg[k].at[first_tile(by_a, 0) + i]

        right, left = {}, {}

        def along_b(by_a):
            right[by_a] = send(whole(by_a, 0), whole(by_a, 0), at_b(1))
            left[by_a] = send(whole(by_a, 0), whole(by_a, 0), at_b(3))

        up = send(whole(0, 0), whole(0, 0), at_a(1))
        down = send(whole(0, 0), whole(0, 0), at_a(3))
        yield
        along_b(0)
        yield
        up.wait_recv()
        relay_up = send(half(3, 0), half(3, 0), at_a(1))
        along_b(3)
        down.wait_recv()
        relay_down = send(half(1, 1), half(1, 1), at_a(3))
        along_b(1)
        yield
        relay_up.wait_recv()
        relay_down.wait_recv()
        along_b(2)
        yield
        relays = []
        for by_a in (0, 3, 1, 2):
            right[by_a].wait_recv()
            if by_a in (0, 1):
                relays.append(send(whole(by_a, 3), whole(by_a, 3), at_b(1)))
            left[by_a].wait_recv()
            if by_a in (2, 3):
                relays.append(send(whole(by_a, 1), whole(by_a, 1), at_b(3)))
        yield
        for copy in relays:
            copy.wait_recv()
        yield

    def reduce_row(k):
        sweep(lambda d: gg[2 * k + 1][d], NN, 5)

        def leaving_core(s):
            bsend[k, :, s] = segment(5, s).reshape(8, 16, TILE).astype(BF16)

        loop(TILES, leaving_core)
        far, nxt, prv, own = (2 * turn(y, by) for by in (2, 1, 3, 0))
        inside = [send(bsend.at[k, pl.ds(b, 2)], cin.at[k, pl.ds(b, 2)], at_core) for b in (far, nxt, prv, own)]
        yield
        sweep(lambda d: gg[2 * k][d], NN, 5)

        def staying(s):
            bown[k, :, s] = segment(5, s).reshape(8, 16, TILE)

        loop(TILES, staying)

        def joined(base):
            for i in range(2):
                def rows(h):
                    cut = pl.ds(h * 8, 8)
                    total = bown[k, base + i, cut] + cin[k, base + i, cut].astype(F32)
                    bown[k, base + i, cut] = total
                    yb[k, base + i, cut] = total.astype(BF16)

                loop(4, rows)

        inside[0].wait_recv()
        joined(far)
        relay_l = send(yb.at[k, far], yrl.at[k], at_y(1))
        relay_r = send(yb.at[k, far + 1], yrr.at[k], at_y(3))
        inside[1].wait_recv()
        joined(nxt)
        plain_l = send(yb.at[k, nxt + 1], yinl.at[k, 1], at_y(1))
        inside[2].wait_recv()
        joined(prv)
        plain_r = send(yb.at[k, prv], yinr.at[k, 0], at_y(3))
        inside[3].wait_recv()
        joined(own)
        yield

        def passed(at, came):
            def rows(h):
                cut = pl.ds(h * 8, 8)
                yb[k, at, cut] = (bown[k, at, cut] + came[k, cut].astype(F32)).astype(BF16)

            loop(4, rows)

        relay_l.wait_recv()
        passed(nxt, yrl)
        sum_l = send(yb.at[k, nxt], yinl.at[k, 0], at_y(1))
        relay_r.wait_recv()
        passed(prv + 1, yrr)
        sum_r = send(yb.at[k, prv + 1], yinr.at[k, 1], at_y(3))
        yield
        for copy in (plain_l, plain_r, sum_l, sum_r):
            copy.wait_recv()

        def total_of(i, cut):
            return bown[k, own + i, cut] + yinl[k, i, cut].astype(F32) + yinr[k, i, cut].astype(F32)

        def leaving(h):
            cut = pl.ds(h * 8, 8)
            zout[k, cut] = total_of(1 - zl, cut).astype(BF16)

        loop(4, leaving)
        to_z = send(zout.at[k], zpin.at[k], at_z)
        yield
        to_z.wait_recv()

        def final(s):
            cut = pl.ds(pl.multiple_of(s * TILE, TILE), TILE)
            gft[16 * k : 16 * k + 16, cut] = (total_of(zl, s) + zpin[k, s].astype(F32)).astype(BF16)

        loop(TILES, final)
        yield

    def reduce_weight():
        rows_y = pl.multiple_of(64 * (y % 2), 64)
        half_y = y // 2
        rows_z = pl.multiple_of(rows_y + 32 * zl, 32)
        rows_x = pl.multiple_of(rows_z + 8 * x, 8)
        lanes = pl.multiple_of(128 * zh, 128)

        def y_part(buffer, by):
            there = turn(y, by)
            return buffer.at[core, there // 2, pl.ds(pl.multiple_of(64 * (there % 2), 64), 64)]

        copy = send(gsum.at[1 - core], rin_c, at_core)
        yield
        copy.wait_recv()
        gsum[core] += rin_c[...]
        copies = [send(y_part(gsum, by), rin_y.at[by - 1], at_y(by)) for by in (1, 2, 3)]
        yield
        for copy in copies:
            copy.wait_recv()
        gsum[core, half_y, pl.ds(rows_y, 64)] += rin_y[0] + rin_y[1] + rin_y[2]
        across_z = pl.ds(pl.multiple_of(rows_y + 32 - 32 * zl, 32), 32)
        copy = send(gsum.at[core, half_y, across_z], rin_z, at_z)
        yield
        copy.wait_recv()
        gsum[core, half_y, pl.ds(rows_z, 32)] += rin_z[...]
        copies = [
            send(
                gsum.at[core, half_y, pl.ds(pl.multiple_of(rows_z + 8 * turn(x, by), 8), 8)],
                rin_x.at[by - 1], at_x(by),
            )
            for by in (1, 2, 3)
        ]
        yield
        for copy in copies:
            copy.wait_recv()
        gsum[core, half_y, pl.ds(rows_x, 8)] += rin_x[0] + rin_x[1] + rin_x[2]
        copies = [
            send(
                gsum.at[core, half_y, pl.ds(rows_x, 8), pl.ds(pl.multiple_of(128 * turn(zh, by), 128), 128)],
                rin_h.at[by - 1], at_h(by),
            )
            for by in (1, 2, 3)
        ]
        yield
        for copy in copies:
            copy.wait_recv()
        corner = (core, half_y, pl.ds(rows_x, 8), pl.ds(lanes, 128))
        gout[corner] = gsum[corner] + rin_h[0] + rin_h[1] + rin_h[2]
        for cut, where in (
            (corner, [at_h(by) for by in (1, 2, 3)]),
            ((core, half_y, pl.ds(rows_x, 8)), [at_x(by) for by in (1, 2, 3)]),
            ((core, half_y, pl.ds(rows_z, 32)), [at_z]),
            ((core, half_y, pl.ds(rows_y, 64)), [at_y(by) for by in (1, 2, 3)]),
            ((core,), [at_core]),
        ):
            copies = [send(gout.at[cut], gout.at[cut], peer) for peer in where]
            yield
            for copy in copies:
                copy.wait_recv()
        for h in range(2):
            for k in range(2):
                gw[:, h, k] = gout[h, k].reshape(8, 16, WIDTH)
        yield

    def go(gen, times=1):
        for _ in range(times):
            next(gen)

    def core_of(q):
        return core if q % 2 == 0 else 1 - core

    def applied(q, cut):
        return dot(aggt[q], weight[:, core_of(q), q // 2, :, cut].reshape(CHUNK, NODES), TN)

    rows = [gather_row(k) for k in range(2)]
    cols = [reduce_col(q, q == 1) for q in range(4)]
    go(rows[0])
    drawn[...] = jnp.zeros((8, TILE), jnp.int32)
    drawn[0:2, 0:SLOTS] = coords[...]
    dest, source = drawn[0:1, :], drawn[1:2, :]
    live = lax.broadcasted_iota(jnp.int32, (1, TILE), 1) < count[0, 0]
    for i, row in enumerate(order_table(dest, source, live) + order_table(source, dest, live)):
        made[i : i + 1, :] = row
    to_table = pltpu.make_async_copy(made, table, local_sem.at[3])
    to_table.start()
    go(rows[0], 2)
    go(rows[1])
    to_table.wait()
    for move in moves:
        move.wait()
    go(rows[0])
    go(cols[0], 2)
    go(rows[1])
    go(rows[0])
    go(cols[1], 2)
    go(rows[1])
    go(cols[0])
    go(rows[1])
    go(cols[2], 2)
    go(cols[0])
    go(rows[1])
    go(cols[3], 2)
    go(cols[2])
    go(cols[1])
    go(cols[0])
    go(cols[0])
    go(cols[2])
    go(cols[1])
    go(cols[3])
    go(cols[2])
    go(cols[1])
    go(cols[3])
    go(cols[2])
    go(cols[1])
    go(cols[3])
    for n in range(2):
        cut = slice(n * NODES, (n + 1) * NODES)
        acted[:, cut] = applied(0, cut) + applied(1, cut) + applied(2, cut)
    go(cols[3])

    for n in range(2):
        cut = slice(n * NODES, (n + 1) * NODES)
        pre = acted[:, cut] + applied(3, cut)
        low = jnp.exp(jnp.minimum(pre, 0.0))
        hid[:, cut] = jnp.where(pre > 0, pre, low - 1.0).astype(BF16)
        slope = jnp.where(pre > 0, 1.0, low)
        gpre[:, cut] = (cot[:, cut].astype(F32) * slope).astype(BF16)

    def grad_agg(q):
        part = dot(weight[:, core_of(q), q // 2].reshape(CHUNK, WIDTH), gpre[...], NT).astype(BF16)
        for i in range(2):
            gg[q][2 * c + i] = part[:, i * TILE : (i + 1) * TILE]

    a, b, d, e = 1, 0, 3, 2
    cols = [gather_col(q, False) for q in range(4)]
    rows = [reduce_row(k) for k in range(2)]
    total = reduce_weight()
    grad_agg(a)
    go(cols[a], 2)
    for q in (b, d, e):
        grad_agg(q)
    for q in range(4):
        gsum[core_of(q), q // 2] = dot(aggt[q], gpre[...], NN)
    go(cols[a])
    go(cols[b])
    go(total)
    go(cols[a])
    go(cols[b], 3)
    go(total)
    go(cols[a])
    go(cols[d], 3)
    go(total)
    go(cols[a])
    go(rows[0])
    go(cols[b])
    go(cols[d])
    go(total)
    go(cols[e], 3)
    go(cols[d])
    go(cols[e])
    go(total)
    go(cols[b])
    go(rows[0])
    go(total)
    go(cols[e])
    go(cols[d])
    go(rows[1])
    go(total)
    go(rows[0])
    go(total)
    go(cols[e])
    go(rows[1])
    go(total)
    go(rows[0])
    go(rows[1])
    go(total)
    go(rows[0])
    go(rows[1])
    go(total)
    go(rows[1])
    for copy in started:
        copy.wait_send()


def hand_over(*refs):
    sources, targets, sems = refs[:3], refs[3:6], refs[6]
    copies = [pltpu.make_async_copy(s, t, sems.at[i]) for i, (s, t) in enumerate(zip(sources, targets))]
    for copy in copies:
        copy.start()
    for copy in copies:
        copy.wait()


def body(node_features, layer_weight, tile_values, tile_coords, tile_count, cotangent):
    vmem = pl.BlockSpec(memory_space=pltpu.VMEM)
    smem = pl.BlockSpec(memory_space=pltpu.SMEM)
    hbm = pl.BlockSpec(memory_space=pl.ANY)
    slab = (CHUNK, TILE)
    bits = (TILES, 16, TILE)
    shapes = [
        jax.ShapeDtypeStruct((NODES, WIDTH), BF16),
        jax.ShapeDtypeStruct((8, 2, 2, 16, WIDTH), F32),
        jax.ShapeDtypeStruct((32, TILES * TILE), BF16),
    ]
    results = pl.pallas_call(
        kernel,
        out_shape=shapes,
        in_specs=[smem, vmem, vmem, hbm, hbm, hbm],
        out_specs=[vmem] * 3,
        scratch_shapes=[
            *[pltpu.VMEM((8,) + bits, BF16)] * 4,
            pltpu.VMEM((SLOTS,) + slab, F32),
            pltpu.VMEM((4, TILES) + slab, BF16),
            pltpu.VMEM((4, 8) + slab, F32),
            pltpu.VMEM((4, 4) + slab, BF16),
            pltpu.VMEM((4, 4) + slab, BF16),
            pltpu.VMEM((4, 8) + slab, BF16),
            pltpu.VMEM((4, 8) + slab, BF16),
            pltpu.VMEM((4, 8) + slab, BF16),
            pltpu.VMEM((4,) + slab, BF16),
            pltpu.VMEM((4,) + slab, BF16),
            pltpu.VMEM((4, 2) + slab, BF16),
            pltpu.VMEM((4, 2) + slab, BF16),
            pltpu.VMEM((4, CHUNK, NODES), BF16),
            pltpu.VMEM((NODES, WIDTH), F32),
            pltpu.VMEM((NODES, WIDTH), BF16),
            *[pltpu.VMEM((TILES,) + slab, BF16)] * 4,
            pltpu.VMEM((2, 8) + bits, F32),
            pltpu.VMEM((2, 8) + bits, BF16),
            pltpu.VMEM((2, 8) + bits, BF16),
            pltpu.VMEM((2, 8) + bits, BF16),
            pltpu.VMEM((2,) + bits, BF16),
            pltpu.VMEM((2,) + bits, BF16),
            pltpu.VMEM((2, 2) + bits, BF16),
            pltpu.VMEM((2, 2) + bits, BF16),
            pltpu.VMEM((2,) + bits, BF16),
            pltpu.VMEM((2,) + bits, BF16),
            pltpu.VMEM((2, 2, 128, WIDTH), F32),
            pltpu.VMEM((2, 2, 128, WIDTH), F32),
            pltpu.VMEM((2, 128, WIDTH), F32),
            pltpu.VMEM((32, WIDTH), F32),
            pltpu.VMEM((3, 64, WIDTH), F32),
            pltpu.VMEM((3, 8, WIDTH), F32),
            pltpu.VMEM((3, 8, 128), F32),
            pltpu.VMEM((SLOTS, TILE, TILE), BF16),
            pltpu.VMEM((8, 2, 2, 16, WIDTH), BF16),
            pltpu.VMEM((NODES, WIDTH), BF16),
            pltpu.VMEM((8, TILE), jnp.int32),
            pltpu.VMEM((16, TILE), jnp.int32),
            pltpu.SMEM((16, TILE), jnp.int32),
            pltpu.SemaphoreType.DMA((WIRES,)),
            pltpu.SemaphoreType.DMA((WIRES,)),
            pltpu.SemaphoreType.DMA((4,)),
        ],
        compiler_params=pltpu.CompilerParams(
            collective_id=0, has_side_effects=True, vmem_limit_bytes=62 * 1024 * 1024
        ),
    )(
        tile_count,
        tile_coords.reshape(SLOTS, 2).T,
        node_features.T,
        tile_values.reshape(SLOTS, TILE, TILE),
        layer_weight.reshape(8, 2, 2, 16, WIDTH),
        cotangent,
    )
    hid, gw, gft = pl.pallas_call(
        hand_over,
        out_shape=shapes,
        in_specs=[vmem] * 3,
        out_specs=[hbm] * 3,
        scratch_shapes=[pltpu.SemaphoreType.DMA((3,))],
    )(*results)
    return hid, gw.reshape(WIDTH, WIDTH), gft.T


def solution(mesh):
    in_specs = (
        P("col", "row"),
        P(),
        P("row", "col", None, None, None),
        P("row", "col", None, None),
        P("row", "col"),
        P(("row", "col"), None),
    )
    out_specs = (P(("row", "col"), None), P(), P("col", "row"))
    return jax.shard_map(body, mesh=mesh, in_specs=in_specs, out_specs=out_specs, check_vma=False)
```

```python
import jax
import jax.numpy as jnp
from jax import lax
from jax.experimental import pallas as pl
from jax.experimental.pallas import tpu as pltpu
from jax.sharding import PartitionSpec as P

MESH = pl.DeviceIdType.MESH
BF16 = jnp.bfloat16
F32 = jnp.float32

SLOTS = 96
TILES = 32
TILE = 128
WIDTH = 512
CHUNK = 128
NODES = 256
UNROLL = 8
WIRES = 208

NT = (((1,), (1,)), ((), ()))
NN = (((1,), (0,)), ((), ()))
TN = (((0,), (0,)), ((), ()))


def dot(a, b, dims):
    return lax.dot_general(a, b, dims, preferred_element_type=F32)


def order_table(main, other, live):
    side = (TILE, TILE)
    lane = lax.broadcasted_iota(jnp.int32, (1, TILE), 1)
    lanes = lax.broadcasted_iota(jnp.int32, side, 1)
    key = jnp.where(live, main * 64 + other, 4096 + lane)
    across = jnp.broadcast_to(key, side)
    down = across.T
    before = down < across
    rank = jnp.sum(before.astype(jnp.int32), axis=0, keepdims=True)
    same = jnp.where(before & ((down >> 6) == (across >> 6)), 1, 0)
    opens = jnp.where(jnp.sum(same, axis=0, keepdims=True) > 0, 0, 1)
    fact = lane + 128 * jnp.where(live, other, 0) + 4096 * opens
    places = jnp.broadcast_to(rank, side).T == lanes
    facts = jnp.sum(jnp.where(places, jnp.broadcast_to(fact, side).T, 0), axis=0, keepdims=True)
    upto = jnp.sum(((down >> 6) <= lanes).astype(jnp.int32), axis=0, keepdims=True)
    count = jnp.sum(((down >> 6) == lanes).astype(jnp.int32), axis=0, keepdims=True)
    return [facts & 127, (facts >> 7) & 31, facts >> 12, jnp.maximum(upto - 1, 0), count]


def kernel(
    count, coords, xin, tiles_hbm, weight_hbm, cot_hbm, hid, gw, gft,
    xg0, xg1, xg2, xg3, run, ys, yown, xrl, xrr, xinl, xinr, zs, zrl, zrr, zinl, zinr,
    aggt, acted, gpre, gg0, gg1, gg2, gg3, bown, bsend, cin, yb, yrl, yrr, yinl, yinr, zout, zpin,
    gsum, gout, rin_c, rin_z, rin_y, rin_x, rin_h, tiles, weight, cot, drawn, made, table,
    send_sem, recv_sem, local_sem,
):
    xg, gg = (xg0, xg1, xg2, xg3), (gg0, gg1, gg2, gg3)
    r = lax.axis_index("row")
    c = lax.axis_index("col")
    y, zl, core = r // 4, (r // 2) % 2, r % 2
    x, zh = c // 4, c % 4

    def turn(v, by):
        return (v + by) % 4

    def at_y(by):
        return (turn(y, by) * 4 + r % 4, c)

    def at_x(by):
        return (r, turn(x, by) * 4 + zh)

    def at_h(by):
        return (r, x * 4 + turn(zh, by))

    at_z = (r + 2 - 4 * zl, c)
    at_core = (r + 1 - 2 * core, c)

    barrier = pltpu.get_barrier_semaphore()
    peers = [at_z, at_core] + [f(by) for f in (at_y, at_x, at_h) for by in (1, 2, 3)]
    for peer in peers:
        pl.semaphore_signal(barrier, inc=1, device_id=peer, device_id_type=MESH)
    moves = [
        pltpu.make_async_copy(src, dst, local_sem.at[i])
        for i, (src, dst) in enumerate(((tiles_hbm, tiles), (weight_hbm, weight), (cot_hbm, cot)))
    ]
    for move in moves:
        move.start()

    def loop(n, f):
        def step(i, carry):
            f(i)
            return carry

        lax.fori_loop(0, n, step, 0)

    place = 2 * y + zl
    place_z = 2 * y + 1 - zl

    def laid_out(s):
        cut = pl.ds(pl.multiple_of(s * TILE, TILE), TILE)
        for k in range(2):
            xg[2 * k][place, s] = xin[16 * k : 16 * k + 16, cut]

    loop(TILES, laid_out)
    pl.semaphore_wait(barrier, len(peers))

    started = []

    def send(src, dst, peer):
        i = len(started)
        copy = pltpu.make_async_remote_copy(
            src_ref=src, dst_ref=dst, send_sem=send_sem.at[i], recv_sem=recv_sem.at[i],
            device_id=peer, device_id_type=MESH,
        )
        copy.start()
        started.append(copy)
        return copy

    def gather_row(k):
        own, across = xg[2 * k], xg[2 * k + 1]

        def part(owner, h):
            return own.at[owner, pl.ds(16 * h, 16)]

        inside = []

        def pass_on(owner):
            inside.append(send(own.at[owner], across.at[owner], at_core))

        def cross(owner, h, peer):
            return send(part(owner, h), part(owner, h), peer)

        to_z = [cross(place, h, at_z) for h in range(2)]
        up = [cross(place, 0, at_y(1)), None]
        down = [None, cross(place, 1, at_y(3))]
        up[1] = cross(place, 1, at_y(1))
        down[0] = cross(place, 0, at_y(3))
        pass_on(place)
        yield
        to_z[0].wait_recv()
        up_z = [cross(place_z, 0, at_y(1)), None]
        to_z[1].wait_recv()
        down_z = [None, cross(place_z, 1, at_y(3))]
        up_z[1] = cross(place_z, 1, at_y(1))
        down_z[0] = cross(place_z, 0, at_y(3))
        pass_on(place_z)
        yield
        relays = []
        for ups, downs, side in ((up, down, zl), (up_z, down_z, 1 - zl)):
            below, above = 2 * turn(y, 3) + side, 2 * turn(y, 1) + side
            ups[0].wait_recv()
            relays.append(cross(below, 0, at_y(1)))
            downs[1].wait_recv()
            relays.append(cross(above, 1, at_y(3)))
        for ups, downs, side in ((up, down, zl), (up_z, down_z, 1 - zl)):
            ups[1].wait_recv()
            pass_on(2 * turn(y, 3) + side)
            downs[0].wait_recv()
            pass_on(2 * turn(y, 1) + side)
        yield
        for side, pair in ((zl, relays[:2]), (1 - zl, relays[2:])):
            for copy in pair:
                copy.wait_recv()
            pass_on(2 * turn(y, 2) + side)
        yield
        for copy in inside:
            copy.wait_recv()
        yield

    def sweep(load, dims, base):
        def step(u, total):
            for v in range(UNROLL):
                t = u * UNROLL + v
                block = tiles[table[base, t]]
                product = dot(load(table[base + 1, t]), block, dims)
                total = jnp.where(table[base + 2, t] > 0, product, total + product)
                run[t] = total
            return total

        lax.fori_loop(0, SLOTS // UNROLL, step, jnp.zeros((CHUNK, TILE), F32))

    def segment(base, d):
        return jnp.where(table[base + 4, d] > 0, run[table[base + 3, d]], 0.0)

    def reduce_col(k, z_first):
        spot_a, spot_b = (zh, x) if z_first else (x, zh)
        at_a, at_b = (at_h, at_x) if z_first else (at_x, at_h)

        def tile_of(base, i):
            return (i // 2) * 8 + base // 4 + i % 2 if z_first else base + i

        sweep(lambda s: xg[k][:, s].reshape(CHUNK, TILE), NT, 0)
        yield
        far, nxt, prv, own = (8 * turn(spot_a, by) for by in (2, 1, 3, 0))

        def rounded(base):
            def one(i):
                ys[k, base + i] = segment(0, tile_of(base, i)).astype(BF16)

            loop(8, one)

        rounded(far)
        relay_l = send(ys.at[k, pl.ds(far, 4)], xrl.at[k], at_a(1))
        relay_r = send(ys.at[k, pl.ds(far + 4, 4)], xrr.at[k], at_a(3))
        rounded(nxt)
        plain_l = send(ys.at[k, pl.ds(nxt + 4, 4)], xinl.at[k, pl.ds(4, 4)], at_a(1))
        rounded(prv)
        plain_r = send(ys.at[k, pl.ds(prv, 4)], xinr.at[k, pl.ds(0, 4)], at_a(3))

        def kept(i):
            yown[k, i] = segment(0, tile_of(own, i))

        loop(8, kept)
        yield

        def passed_l(i):
            ys[k, nxt + i] = (ys[k, nxt + i].astype(F32) + xrl[k, i].astype(F32)).astype(BF16)

        def passed_r(i):
            ys[k, prv + 4 + i] = (ys[k, prv + 4 + i].astype(F32) + xrr[k, i].astype(F32)).astype(BF16)

        relay_l.wait_recv()
        loop(4, passed_l)
        sum_l = send(ys.at[k, pl.ds(nxt, 4)], xinl.at[k, pl.ds(0, 4)], at_a(1))
        relay_r.wait_recv()
        loop(4, passed_r)
        sum_r = send(ys.at[k, pl.ds(prv + 4, 4)], xinr.at[k, pl.ds(4, 4)], at_a(3))
        yield
        for copy in (plain_l, plain_r, sum_l, sum_r):
            copy.wait_recv()

        def summed(i):
            total = yown[k, i] + xinl[k, i].astype(F32) + xinr[k, i].astype(F32)
            yown[k, i] = total
            zs[k, i] = total.astype(BF16)

        loop(8, summed)
        far, nxt, prv, own = (2 * turn(spot_b, by) for by in (2, 1, 3, 0))
        relay_l = send(zs.at[k, far], zrl.at[k], at_b(1))
        relay_r = send(zs.at[k, far + 1], zrr.at[k], at_b(3))
        plain_l = send(zs.at[k, nxt + 1], zinl.at[k, 1], at_b(1))
        plain_r = send(zs.at[k, prv], zinr.at[k, 0], at_b(3))
        yield
        relay_l.wait_recv()
        zs[k, nxt] = (yown[k, nxt] + zrl[k].astype(F32)).astype(BF16)
        sum_l = send(zs.at[k, nxt], zinl.at[k, 0], at_b(1))
        relay_r.wait_recv()
        zs[k, prv + 1] = (yown[k, prv + 1] + zrr[k].astype(F32)).astype(BF16)
        sum_r = send(zs.at[k, prv + 1], zinr.at[k, 1], at_b(3))
        yield
        for copy in (plain_l, plain_r, sum_l, sum_r):
            copy.wait_recv()
        for i in range(2):
            total = yown[k, own + i] + zinl[k, i].astype(F32) + zinr[k, i].astype(F32)
            aggt[k, :, i * TILE : (i + 1) * TILE] = total.astype(BF16)
        yield

    def gather_col(k, x_first):
        at_a, at_b = (at_x, at_h) if x_first else (at_h, at_x)

        def first_tile(by_a, by_b):
            by_x, by_h = (by_a, by_b) if x_first else (by_b, by_a)
            return 2 * (turn(x, by_x) * 4 + turn(zh, by_h))

        def whole(by_a, by_b):
            return gg[k].at[pl.ds(first_tile(by_a, by_b), 2)]

        def half(by_a, i):
            return gg[k].at[first_tile(by_a, 0) + i]

        right, left = {}, {}

        def along_b(by_a):
            right[by_a] = send(whole(by_a, 0), whole(by_a, 0), at_b(1))
            left[by_a] = send(whole(by_a, 0), whole(by_a, 0), at_b(3))

        up = send(whole(0, 0), whole(0, 0), at_a(1))
        down = send(whole(0, 0), whole(0, 0), at_a(3))
        yield
        along_b(0)
        yield
        up.wait_recv()
        relay_up = send(half(3, 0), half(3, 0), at_a(1))
        along_b(3)
        down.wait_recv()
        relay_down = send(half(1, 1), half(1, 1), at_a(3))
        along_b(1)
        yield
        relay_up.wait_recv()
        relay_down.wait_recv()
        along_b(2)
        yield
        relays = []
        for by_a in (0, 3, 1, 2):
            right[by_a].wait_recv()
            if by_a in (0, 1):
                relays.append(send(whole(by_a, 3), whole(by_a, 3), at_b(1)))
            left[by_a].wait_recv()
            if by_a in (2, 3):
                relays.append(send(whole(by_a, 1), whole(by_a, 1), at_b(3)))
        yield
        for copy in relays:
            copy.wait_recv()
        yield

    def reduce_row(k):
        sweep(lambda d: gg[2 * k + 1][d], NN, 5)

        def leaving_core(s):
            bsend[k, :, s] = segment(5, s).reshape(8, 16, TILE).astype(BF16)

        loop(TILES, leaving_core)
        far, nxt, prv, own = (2 * turn(y, by) for by in (2, 1, 3, 0))
        inside = [send(bsend.at[k, pl.ds(b, 2)], cin.at[k, pl.ds(b, 2)], at_core) for b in (far, nxt, prv, own)]
        yield
        sweep(lambda d: gg[2 * k][d], NN, 5)

        def staying(s):
            bown[k, :, s] = segment(5, s).reshape(8, 16, TILE)

        loop(TILES, staying)

        def joined(base):
            for i in range(2):
                def rows(h):
                    cut = pl.ds(h * 8, 8)
                    total = bown[k, base + i, cut] + cin[k, base + i, cut].astype(F32)
                    bown[k, base + i, cut] = total
                    yb[k, base + i, cut] = total.astype(BF16)

                loop(4, rows)

        def half(h):
            return pl.ds(16 * h, 16)

        inside[0].wait_recv()
        joined(far)
        relay_l, relay_r = [], []
        for h in range(2):
            relay_l.append(send(yb.at[k, far, half(h)], yrl.at[k, half(h)], at_y(1)))
            relay_r.append(send(yb.at[k, far + 1, half(h)], yrr.at[k, half(h)], at_y(3)))
        inside[1].wait_recv()
        joined(nxt)
        plain_l = send(yb.at[k, nxt + 1], yinl.at[k, 1], at_y(1))
        inside[2].wait_recv()
        joined(prv)
        plain_r = send(yb.at[k, prv], yinr.at[k, 0], at_y(3))
        inside[3].wait_recv()
        joined(own)
        yield

        def passed(at, came, h):
            def rows(g):
                cut = pl.ds(16 * h + g * 8, 8)
                yb[k, at, cut] = (bown[k, at, cut] + came[k, cut].astype(F32)).astype(BF16)

            loop(2, rows)

        sum_l, sum_r = [], []
        for h in range(2):
            relay_l[h].wait_recv()
            passed(nxt, yrl, h)
            sum_l.append(send(yb.at[k, nxt, half(h)], yinl.at[k, 0, half(h)], at_y(1)))
            relay_r[h].wait_recv()
            passed(prv + 1, yrr, h)
            sum_r.append(send(yb.at[k, prv + 1, half(h)], yinr.at[k, 1, half(h)], at_y(3)))
        yield
        plain_l.wait_recv()
        plain_r.wait_recv()

        def total_of(i, cut):
            return bown[k, own + i, cut] + yinl[k, i, cut].astype(F32) + yinr[k, i, cut].astype(F32)

        to_z = []
        for h in range(2):
            sum_l[h].wait_recv()
            sum_r[h].wait_recv()

            def leaving(g):
                cut = pl.ds(16 * h + g * 8, 8)
                zout[k, cut] = total_of(1 - zl, cut).astype(BF16)

            loop(2, leaving)
            to_z.append(send(zout.at[k, half(h)], zpin.at[k, half(h)], at_z))
        yield
        for copy in to_z:
            copy.wait_recv()

        def final(s):
            cut = pl.ds(pl.multiple_of(s * TILE, TILE), TILE)
            gft[16 * k : 16 * k + 16, cut] = (total_of(zl, s) + zpin[k, s].astype(F32)).astype(BF16)

        loop(TILES, final)
        yield

    def reduce_weight():
        rows_y = pl.multiple_of(64 * (y % 2), 64)
        half_y = y // 2
        rows_z = pl.multiple_of(rows_y + 32 * zl, 32)
        rows_x = pl.multiple_of(rows_z + 8 * x, 8)

        def y_part(buffer, by):
            there = turn(y, by)
            return buffer.at[core, there // 2, pl.ds(pl.multiple_of(64 * (there % 2), 64), 64)]

        copy = send(gsum.at[1 - core], rin_c, at_core)
        yield
        copy.wait_recv()
        gsum[core] += rin_c[...]
        copies = [send(y_part(gsum, by), rin_y.at[by - 1], at_y(by)) for by in (1, 2, 3)]
        yield
        for copy in copies:
            copy.wait_recv()
        gsum[core, half_y, pl.ds(rows_y, 64)] += rin_y[0] + rin_y[1] + rin_y[2]
        across_z = pl.ds(pl.multiple_of(rows_y + 32 - 32 * zl, 32), 32)
        copy = send(gsum.at[core, half_y, across_z], rin_z, at_z)
        yield
        copy.wait_recv()
        gsum[core, half_y, pl.ds(rows_z, 32)] += rin_z[...]
        copies = [
            send(
                gsum.at[core, half_y, pl.ds(pl.multiple_of(rows_z + 8 * turn(x, by), 8), 8)],
                rin_x.at[by - 1], at_x(by),
            )
            for by in (1, 2, 3)
        ]
        yield
        for copy in copies:
            copy.wait_recv()
        gsum[core, half_y, pl.ds(rows_x, 8)] += rin_x[0] + rin_x[1] + rin_x[2]
        rin_h[zh] = gsum[core, half_y, pl.ds(rows_x, 8)]
        copies = [send(rin_h.at[zh], rin_h.at[zh], at_h(by)) for by in (1, 2, 3)]
        yield
        for copy in copies:
            copy.wait_recv()
        gout[core, half_y, pl.ds(rows_x, 8)] = (rin_h[0] + rin_h[1]) + (rin_h[2] + rin_h[3])
        for cut, where in (
            ((core, half_y, pl.ds(rows_x, 8)), [at_x(by) for by in (1, 2, 3)]),
            ((core, half_y, pl.ds(rows_z, 32)), [at_z]),
            ((core, half_y, pl.ds(rows_y, 64)), [at_y(by) for by in (1, 2, 3)]),
            ((core,), [at_core]),
        ):
            copies = [send(gout.at[cut], gout.at[cut], peer) for peer in where]
            yield
            for copy in copies:
                copy.wait_recv()
        for h in range(2):
            for k in range(2):
                gw[:, h, k] = gout[h, k].reshape(8, 16, WIDTH)
        yield

    def go(gen, times=1):
        for _ in range(times):
            next(gen)

    def core_of(q):
        return core if q % 2 == 0 else 1 - core

    def applied(q, cut):
        return dot(aggt[q], weight[:, core_of(q), q // 2, :, cut].reshape(CHUNK, NODES), TN)

    rows = [gather_row(k) for k in range(2)]
    cols = [reduce_col(q, q == 1) for q in range(4)]
    go(rows[0])
    drawn[...] = jnp.zeros((8, TILE), jnp.int32)
    drawn[0:2, 0:SLOTS] = coords[...]
    dest, source = drawn[0:1, :], drawn[1:2, :]
    live = lax.broadcasted_iota(jnp.int32, (1, TILE), 1) < count[0, 0]
    for i, row in enumerate(order_table(dest, source, live) + order_table(source, dest, live)):
        made[i : i + 1, :] = row
    to_table = pltpu.make_async_copy(made, table, local_sem.at[3])
    to_table.start()
    go(rows[0], 2)
    go(rows[1])
    to_table.wait()
    for move in moves:
        move.wait()
    go(rows[0])
    go(cols[0], 2)
    go(rows[1])
    go(rows[0])
    go(cols[1], 2)
    go(rows[1])
    go(cols[0])
    go(rows[1])
    go(cols[2], 2)
    go(cols[0])
    go(rows[1])
    go(cols[3], 2)
    go(cols[2])
    go(cols[1])
    go(cols[0])
    go(cols[0])
    go(cols[2])
    go(cols[1])
    go(cols[3])
    go(cols[2])
    go(cols[1])
    go(cols[3])
    go(cols[2])
    go(cols[1])
    go(cols[3])
    for n in range(2):
        cut = slice(n * NODES, (n + 1) * NODES)
        acted[:, cut] = applied(0, cut) + applied(1, cut) + applied(2, cut)
    go(cols[3])

    for n in range(2):
        cut = slice(n * NODES, (n + 1) * NODES)
        pre = acted[:, cut] + applied(3, cut)
        low = jnp.exp(jnp.minimum(pre, 0.0))
        hid[:, cut] = jnp.where(pre > 0, pre, low - 1.0).astype(BF16)
        slope = jnp.where(pre > 0, 1.0, low)
        gpre[:, cut] = (cot[:, cut].astype(F32) * slope).astype(BF16)

    def grad_agg(q):
        part = dot(weight[:, core_of(q), q // 2].reshape(CHUNK, WIDTH), gpre[...], NT).astype(BF16)
        for i in range(2):
            gg[q][2 * c + i] = part[:, i * TILE : (i + 1) * TILE]

    a, b, d, e = 1, 0, 3, 2
    cols = [gather_col(q, False) for q in range(4)]
    rows = [reduce_row(k) for k in range(2)]
    total = reduce_weight()
    grad_agg(a)
    go(cols[a], 2)
    for q in (b, d, e):
        grad_agg(q)
    for q in range(4):
        gsum[core_of(q), q // 2] = dot(aggt[q], gpre[...], NN)
    go(cols[a])
    go(cols[b])
    go(total)
    go(cols[a])
    go(cols[b], 3)
    go(total)
    go(cols[a])
    go(cols[d], 3)
    go(total)
    go(cols[a])
    go(rows[0])
    go(cols[b])
    go(cols[d])
    go(total)
    go(cols[e], 3)
    go(cols[d])
    go(cols[e])
    go(total)
    go(cols[b])
    go(rows[0])
    go(total)
    go(cols[e])
    go(cols[d])
    go(rows[1])
    go(total)
    go(rows[0])
    go(total)
    go(cols[e])
    go(rows[1])
    go(total)
    go(rows[0])
    go(rows[1])
    go(total)
    go(rows[0])
    go(rows[1])
    go(rows[1])
    for copy in started:
        copy.wait_send()


def hand_over(*refs):
    sources, targets, sems = refs[:3], refs[3:6], refs[6]
    copies = [pltpu.make_async_copy(s, t, sems.at[i]) for i, (s, t) in enumerate(zip(sources, targets))]
    for copy in copies:
        copy.start()
    for copy in copies:
        copy.wait()


def body(node_features, layer_weight, tile_values, tile_coords, tile_count, cotangent):
    vmem = pl.BlockSpec(memory_space=pltpu.VMEM)
    smem = pl.BlockSpec(memory_space=pltpu.SMEM)
    hbm = pl.BlockSpec(memory_space=pl.ANY)
    slab = (CHUNK, TILE)
    bits = (TILES, 16, TILE)
    shapes = [
        jax.ShapeDtypeStruct((NODES, WIDTH), BF16),
        jax.ShapeDtypeStruct((8, 2, 2, 16, WIDTH), F32),
        jax.ShapeDtypeStruct((32, TILES * TILE), BF16),
    ]
    results = pl.pallas_call(
        kernel,
        out_shape=shapes,
        in_specs=[smem, vmem, vmem, hbm, hbm, hbm],
        out_specs=[vmem] * 3,
        scratch_shapes=[
            *[pltpu.VMEM((8,) + bits, BF16)] * 4,
            pltpu.VMEM((SLOTS,) + slab, F32),
            pltpu.VMEM((4, TILES) + slab, BF16),
            pltpu.VMEM((4, 8) + slab, F32),
            pltpu.VMEM((4, 4) + slab, BF16),
            pltpu.VMEM((4, 4) + slab, BF16),
            pltpu.VMEM((4, 8) + slab, BF16),
            pltpu.VMEM((4, 8) + slab, BF16),
            pltpu.VMEM((4, 8) + slab, BF16),
            pltpu.VMEM((4,) + slab, BF16),
            pltpu.VMEM((4,) + slab, BF16),
            pltpu.VMEM((4, 2) + slab, BF16),
            pltpu.VMEM((4, 2) + slab, BF16),
            pltpu.VMEM((4, CHUNK, NODES), BF16),
            pltpu.VMEM((NODES, WIDTH), F32),
            pltpu.VMEM((NODES, WIDTH), BF16),
            *[pltpu.VMEM((TILES,) + slab, BF16)] * 4,
            pltpu.VMEM((2, 8) + bits, F32),
            pltpu.VMEM((2, 8) + bits, BF16),
            pltpu.VMEM((2, 8) + bits, BF16),
            pltpu.VMEM((2, 8) + bits, BF16),
            pltpu.VMEM((2,) + bits, BF16),
            pltpu.VMEM((2,) + bits, BF16),
            pltpu.VMEM((2, 2) + bits, BF16),
            pltpu.VMEM((2, 2) + bits, BF16),
            pltpu.VMEM((2,) + bits, BF16),
            pltpu.VMEM((2,) + bits, BF16),
            pltpu.VMEM((2, 2, 128, WIDTH), F32),
            pltpu.VMEM((2, 2, 128, WIDTH), F32),
            pltpu.VMEM((2, 128, WIDTH), F32),
            pltpu.VMEM((32, WIDTH), F32),
            pltpu.VMEM((3, 64, WIDTH), F32),
            pltpu.VMEM((3, 8, WIDTH), F32),
            pltpu.VMEM((4, 8, WIDTH), F32),
            pltpu.VMEM((SLOTS, TILE, TILE), BF16),
            pltpu.VMEM((8, 2, 2, 16, WIDTH), BF16),
            pltpu.VMEM((NODES, WIDTH), BF16),
            pltpu.VMEM((8, TILE), jnp.int32),
            pltpu.VMEM((16, TILE), jnp.int32),
            pltpu.SMEM((16, TILE), jnp.int32),
            pltpu.SemaphoreType.DMA((WIRES,)),
            pltpu.SemaphoreType.DMA((WIRES,)),
            pltpu.SemaphoreType.DMA((4,)),
        ],
        compiler_params=pltpu.CompilerParams(
            collective_id=0, has_side_effects=True, vmem_limit_bytes=62 * 1024 * 1024
        ),
    )(
        tile_count,
        tile_coords.reshape(SLOTS, 2).T,
        node_features.T,
        tile_values.reshape(SLOTS, TILE, TILE),
        layer_weight.reshape(8, 2, 2, 16, WIDTH),
        cotangent,
    )
    hid, gw, gft = pl.pallas_call(
        hand_over,
        out_shape=shapes,
        in_specs=[vmem] * 3,
        out_specs=[hbm] * 3,
        scratch_shapes=[pltpu.SemaphoreType.DMA((3,))],
    )(*results)
    return hid, gw.reshape(WIDTH, WIDTH), gft.T


def solution(mesh):
    in_specs = (
        P("col", "row"),
        P(),
        P("row", "col", None, None, None),
        P("row", "col", None, None),
        P("row", "col"),
        P(("row", "col"), None),
    )
    out_specs = (P(("row", "col"), None), P(), P("col", "row"))
    return jax.shard_map(body, mesh=mesh, in_specs=in_specs, out_specs=out_specs, check_vma=False)
```
